256 devices in a mesh: date: 16 (over z, core), strip: 16 (over y, x).
Axes of the slice: x: 4, y: 4, z: 8, core: 2. Of those that a mesh axis runs over, the one named last changes fastest.
Arguments:
- images: bfloat16 [2, 64, 1280, 5120], P(None, 'date', 'strip'), as said below
- date_pairs: int32 [128, 2], replicated, may hold values from 0 to 63, as said below
- assignment: int32 [128], replicated, may hold values from 0 to 255, as said below
Outputs:
- coherence: float32 [2, 256, 65536], P(None, 'date', 'strip')
- date_sums: float32 [2, 64, 65536], P(None, 'date', 'strip')
The draws below stay inside these ranges and needn't reach their ends.
Inputs may be any that keep to these rules, and one draw needn't show every extreme that they name: `date_pairs`: each row holds two different dates at most 4 apart, and no ordered pair of dates is listed twice. Rows whose first date lies in one aligned block of 4 dates number at most 16, and exactly that many in some block. `assignment`: rows are distinct. The rows r with r // 16 equal to o belong to owner o; within them, consecutive groups of 1 row hold, in order, only pairs whose first date lies in the 0th, 1st, ... aligned block of 4 dates. In some owner's rows every group is full. `images`: values stay finite and of moderate size; every pixel is nonzero with probability one.
All inputs are finite; a program needn't handle non-finite values.
Results may differ from the reference program's by a relative error of at most 0.00084.
Values may be sent and summed in bfloat16 or wider, within the bound.
No kernel may reach another device: no remote copies, remote signals or barrier semaphores. Data moves between devices by JAX's collectives and lax.ppermute only.
A program may use at most 256 MiB of HBM per device.

```python
import math
import jax
import jax.numpy as jnp
from jax import lax

DATES_DEV = 4
RG = 5120
PAIR_DEV = 8
BASE = 4
ALOOK = 5
RLOOK = 20
DATES = 64
AZ = 1280
PAIRS = 128
ROWS = 256
CELLS = 65536


def pair_tables(key):
    key = jax.random.fold_in(key, 7)
    keys = jax.random.split(key, 7)
    blocks = PAIRS // PAIR_DEV
    half = PAIR_DEV // 2
    position = jnp.arange(blocks)
    offset_pos = position - 3
    magnitude = jax.random.randint(keys[0], (blocks,), 0, half)
    previous = magnitude[jnp.clip(position - 1, 0, blocks - 1)]
    paired_up = jnp.where(position + 1 < blocks, magnitude, 0)
    delta = jnp.where(position == 0, PAIR_DEV, jnp.where(position < 3, -half, jnp.where(offset_pos % 2 == 0, paired_up, -previous)))
    shuffle = jax.random.permutation(keys[1], blocks)
    shuffle = (shuffle - shuffle[0] + blocks - 1) % blocks
    counts = jnp.zeros((blocks,), jnp.int32).at[shuffle].set((PAIR_DEV + delta).astype(jnp.int32))
    ends = jnp.cumsum(counts)
    starts = ends - counts
    index = jnp.arange(PAIRS)
    block_of = jnp.sum((index[:, None] >= ends[None, :]).astype(jnp.int32), axis=1)
    within = index - starts[block_of]
    choices_all = DATES_DEV * 2 * BASE
    candidate = jnp.arange(choices_all)
    cand_offset = candidate // (2 * BASE)
    cand_kind = candidate % (2 * BASE)
    cand_sign = jnp.where(cand_kind < BASE, 1, -1)
    cand_dist = cand_kind % BASE + 1
    cand_first = jnp.arange(blocks)[:, None] * DATES_DEV + cand_offset[None, :]
    cand_second = cand_first + (cand_sign * cand_dist)[None, :]
    valid = (cand_second >= 0) & (cand_second < DATES)
    scores = jax.random.randint(keys[5], (blocks, choices_all), 0, 2 ** 16) * choices_all + candidate[None, :]
    scores = jnp.where(valid, scores, scores + 2 ** 28)
    scores = scores.at[0, BASE - 1].set(-1)
    scores = scores.at[blocks - 1, choices_all - 1].set(-1)
    ranking = jnp.argsort(scores, axis=1, stable=True)
    picked = ranking[block_of, within]
    first_date = cand_first[block_of, picked]
    second_date = cand_second[block_of, picked]
    owner_scores = jax.random.randint(keys[2], (blocks, blocks), 0, 2 ** 20) * blocks + jnp.arange(blocks)[None, :]
    owner_scores = owner_scores.at[0, 0].set(-1)
    sigma = jnp.argsort(owner_scores, axis=1, stable=True)
    owner = sigma[block_of, within % blocks]
    rank = within // blocks
    per_owner = 2 * PAIR_DEV // blocks
    row_index = owner * 2 * PAIR_DEV + block_of * per_owner + rank
    order = jax.random.permutation(keys[6], PAIRS)
    pairs_out = jnp.stack([first_date, second_date], axis=1)[order].astype(jnp.int32)
    return (pairs_out, row_index[order].astype(jnp.int32))


def draw_date_pairs(key, part):
    return pair_tables(key)[0]


def draw_assignment(key, part):
    return pair_tables(key)[1]


def draw_images(key, part):
    keys = jax.random.split(jax.random.fold_in(key, 11), 5)
    columns = jnp.arange(RG, dtype=jnp.float32) / RG
    amplitude = jnp.exp(jax.random.uniform(keys[0], (AZ, RG), jnp.float32, -1.0, 1.0))
    ramp = jax.random.uniform(keys[1], (DATES, 1, 1), jnp.float32, -6.0, 6.0)
    start = jax.random.uniform(keys[2], (DATES, 1, 1), jnp.float32, -math.pi, math.pi)
    jitter = 0.5 * jax.random.normal(keys[3], (DATES, AZ, RG), jnp.float32)
    theta = start + ramp * columns[None, None, :] + jitter
    noise = 0.6 * jax.random.normal(keys[4], (2, DATES, AZ, RG), jnp.float32)
    signal = jnp.stack([jnp.cos(theta), jnp.sin(theta)])
    return (amplitude[None, None] * (signal + noise)).astype(jnp.bfloat16)


def setup_inputs(seed: int = 0) -> dict:
    seeds = jax.random.split(jax.random.key(seed), 4)
    images = draw_images(jax.random.fold_in(seeds[3], 71), 0)
    date_pairs = draw_date_pairs(jax.random.fold_in(seeds[3], 71), 0)
    assignment = draw_assignment(jax.random.fold_in(seeds[3], 71), 0)
    return dict(images=images, date_pairs=date_pairs, assignment=assignment)


eps_power = 1e-06

def looks(values):
    shaped = values.reshape(values.shape[:-2] + (AZ // ALOOK, ALOOK, RG // RLOOK, RLOOK))
    return lax.optimization_barrier(jnp.sum(shaped, axis=(-3, -1)))

def smooth_rows(looked):
    widths = [(0, 0)] * (looked.ndim - 2) + [(1, 1), (0, 0)]
    padded = jnp.pad(looked, widths)
    return padded[..., :-2, :] + 2.0 * padded[..., 1:-1, :] + padded[..., 2:, :]

def reference(images, date_pairs, assignment):

    def power_of(date_index):
        picture = lax.dynamic_index_in_dim(images, date_index, 1, keepdims=False)
        squared = (jnp.square(picture[0].astype(jnp.float32)) + jnp.square(picture[1].astype(jnp.float32))).astype(jnp.bfloat16)
        squared = lax.optimization_barrier(squared)
        return smooth_rows(looks(squared.astype(jnp.float32)))
    powers = lax.map(power_of, jnp.arange(DATES, dtype=jnp.int32))

    def pair_of(pair_row):
        front_image = lax.dynamic_index_in_dim(images, pair_row[0], 1, keepdims=False).astype(jnp.float32)
        back_image = lax.dynamic_index_in_dim(images, pair_row[1], 1, keepdims=False).astype(jnp.float32)
        cross_real = front_image[0] * back_image[0] + front_image[1] * back_image[1]
        cross_imag = front_image[1] * back_image[0] - front_image[0] * back_image[1]
        cross = jnp.stack([cross_real, cross_imag]).astype(jnp.bfloat16)
        cross = lax.optimization_barrier(cross)
        smoothed = smooth_rows(looks(cross.astype(jnp.float32)))
        scale = lax.rsqrt(powers[pair_row[0]] * powers[pair_row[1]] + eps_power)
        return smoothed * scale[None]
    coh_all = lax.map(pair_of, date_pairs)
    flat = jnp.moveaxis(coh_all, 1, 0).reshape(2, PAIRS, CELLS)
    coherence = jnp.zeros((2, ROWS, CELLS), jnp.float32).at[:, assignment].set(flat)
    sums = jnp.zeros((2, DATES, CELLS), jnp.float32)
    sums = sums.at[0, date_pairs[:, 0]].add(flat[0]).at[1, date_pairs[:, 0]].add(flat[1])
    sums = sums.at[0, date_pairs[:, 1]].add(flat[0]).at[1, date_pairs[:, 1]].add(-flat[1])
    return (coherence, sums)
```

```python
import functools

import jax
import jax.numpy as jnp
from jax import lax
from jax.experimental import pallas as pl
from jax.experimental.pallas import tpu as pltpu
from jax.sharding import PartitionSpec as P

ALOOK = 5
RLOOK = 20
LANES = 128
EPS_POWER = 1e-06

INNER = ((2, 3), (2, 4), (2, 5), (3, 4), (3, 5), (4, 5))
LOWER = ((0, 4), (1, 4), (1, 5), (1, 2), (1, 3))
UPPER = ((2, 6), (3, 6), (3, 7), (4, 6), (4, 7))
FORMED = INNER + LOWER + UPPER
FROM_BELOW = tuple((i - 4, j - 4) for i, j in UPPER)
FROM_ABOVE = tuple((i + 4, j + 4) for i, j in LOWER)
KNOWN = FORMED + FROM_BELOW + FROM_ABOVE
COLUMNS = 1280


def products_kernel(edges, powers, counts, *refs):
    sources = refs[: len(counts)]
    look_ref, out_ref, planes_ref, acc_ref = refs[len(counts) :]
    rows, width = sources[0].shape[2], sources[0].shape[3]
    total = 2 * len(edges) + len(powers)
    step = pl.program_id(0)
    places = {}
    for source, start in zip(sources, counts):
        for n in range(source.shape[1]):
            places[start + n] = (source, n)
    used = sorted({k for e in edges for k in e} | set(powers))
    tiles = rows // 16

    def form(index, _):
        row = pl.multiple_of(index % tiles * 16, 16)
        lane = pl.multiple_of(index // tiles * LANES, LANES)
        pixel = {}
        for k in used:
            source, n = places[k]
            pixel[k] = tuple(
                source[c, n, pl.ds(row, 16), pl.ds(lane, LANES)].astype(jnp.float32) for c in (0, 1)
            )
        results = []
        for i, j in edges:
            results.append(pixel[i][0] * pixel[j][0] + pixel[i][1] * pixel[j][1])
        for i, j in edges:
            results.append(pixel[i][1] * pixel[j][0] - pixel[i][0] * pixel[j][1])
        for k in powers:
            results.append(pixel[k][0] * pixel[k][0] + pixel[k][1] * pixel[k][1])
        for p, value in enumerate(results):
            planes_ref[pl.ds(p * rows + row, 16), pl.ds(lane, LANES)] = value.astype(jnp.bfloat16)
        return 0

    lax.fori_loop(0, tiles * (width // LANES), form, 0)
    group = 4 if total % 4 == 0 else 2
    for g in range(total // group):
        span = pl.ds(g * group * rows, group * rows)
        part = jnp.dot(planes_ref[span, :], look_ref[...], preferred_element_type=jnp.float32)

        @pl.when(step % 2 == 0)
        def _():
            acc_ref[span, :] = part

        @pl.when(step % 2 == 1)
        def _():
            acc_ref[span, :] += part

    @pl.when(step % 2 == 1)
    def _():
        for m in range(rows // ALOOK):
            for p in range(0, total, 8):
                size = min(8, total - p)
                value = acc_ref[pl.ds(p * rows + m * ALOOK, size, stride=rows), :]
                for k in range(1, ALOOK):
                    value += acc_ref[pl.ds(p * rows + m * ALOOK + k, size, stride=rows), :]
                out_ref[m, p : p + size, :] = value


def looked_products(edges, powers, sources, counts, look_matrix):
    rows, columns = sources[0].shape[2], sources[0].shape[3]
    total = 2 * len(edges) + len(powers)
    cells = rows // ALOOK
    return pl.pallas_call(
        functools.partial(products_kernel, edges, powers, counts),
        out_shape=jax.ShapeDtypeStruct((cells, total, columns // RLOOK), jnp.float32),
        grid=(columns // COLUMNS,),
        in_specs=[
            pl.BlockSpec((2, s.shape[1], rows, COLUMNS), lambda i: (0, 0, 0, i)) for s in sources
        ]
        + [pl.BlockSpec((COLUMNS, LANES), lambda i: (i % 2, 0))],
        out_specs=pl.BlockSpec((cells, total, LANES), lambda i: (0, 0, i // 2)),
        scratch_shapes=[
            pltpu.VMEM((total * rows, COLUMNS), jnp.bfloat16),
            pltpu.VMEM((total * rows, LANES), jnp.float32),
        ],
        compiler_params=pltpu.CompilerParams(vmem_limit_bytes=48 * 2**20),
    )(*sources, look_matrix)


def coherence_kernel(inner_ref, outer_ref, inner_before, outer_before, inner_after, outer_after, own_ref, low_ref, up_ref):
    cells = inner_ref.shape[0]
    n_in, n_out = len(INNER), len(LOWER) + len(UPPER)
    n_low = len(LOWER)

    def at(ref, before, after, m):
        if m < 0:
            return before[0]
        if m >= cells:
            return after[0]
        return ref[m]

    for m in range(cells):
        smooth = []
        for ref, before, after in (
            (inner_ref, inner_before, inner_after),
            (outer_ref, outer_before, outer_after),
        ):
            smooth.append(
                at(ref, before, after, m - 1) + 2.0 * ref[m] + at(ref, before, after, m + 1)
            )
        inner, outer = smooth
        power = {2 + k: inner[2 * n_in + k : 2 * n_in + k + 1] for k in range(4)}
        for k, place in enumerate((0, 1, 6, 7)):
            power[place] = outer[2 * n_out + k : 2 * n_out + k + 1]

        def scaled(values, edges, start, count):
            first = jnp.concatenate([power[i] for i, _ in edges], axis=0)
            second = jnp.concatenate([power[j] for _, j in edges], axis=0)
            scale = lax.rsqrt(first * second + EPS_POWER)
            return values[start : start + len(edges)] * scale, values[
                start + count : start + count + len(edges)
            ] * scale

        re, im = scaled(inner, INNER, 0, n_in)
        own_ref[m, 0:n_in, :] = re
        own_ref[m, n_in : 2 * n_in, :] = im
        re, im = scaled(outer, LOWER, 0, n_out)
        low_ref[m, 0:n_low, :] = re
        low_ref[m, n_low : 2 * n_low, :] = im
        re, im = scaled(outer, UPPER, n_low, n_out)
        up_ref[m, 0:n_low, :] = re
        up_ref[m, n_low : 2 * n_low, :] = im


def coherences(inner, outer, inner_halo, outer_halo):
    cells, _, width = inner.shape
    shapes = [2 * len(INNER), 2 * len(LOWER), 2 * len(UPPER)]
    full = lambda a: pl.BlockSpec(a.shape, lambda: (0,) * len(a.shape))
    args = (inner, outer, inner_halo[0], outer_halo[0], inner_halo[1], outer_halo[1])
    return pl.pallas_call(
        coherence_kernel,
        out_shape=[jax.ShapeDtypeStruct((cells, n, width), jnp.float32) for n in shapes],
        in_specs=[full(a) for a in args],
        out_specs=[
            pl.BlockSpec((cells, n, width), lambda: (0, 0, 0)) for n in shapes
        ],
        compiler_params=pltpu.CompilerParams(vmem_limit_bytes=32 * 2**20),
    )(*args)


def select_kernel(slot_ref, sign_ref, count_ref, own, low, up, below, above, slots_ref, sums_ref):
    cells, _, width = own.shape
    tables = (own, low, up, below, above)
    lengths = (len(INNER), len(LOWER), len(UPPER), len(UPPER), len(LOWER))
    pick_index = []

    owners = slots_ref.shape[0] // (2 * cells * width // LANES)
    known = len(KNOWN)
    one_hot = []
    hot_im = []
    lanes = lax.broadcasted_iota(jnp.int32, (1, known), 1)
    for o in range(owners):
        hit = (lanes == slot_ref[o]).astype(jnp.float32)
        one_hot.append(hit)
        hot_im.append(hit * sign_ref[o])
    weight_re, weight_im = [], []
    for k in range(2, 6):
        row_re = jnp.zeros((1, known), jnp.float32)
        row_im = jnp.zeros((1, known), jnp.float32)
        for e, (i, j) in enumerate(KNOWN):
            if k in (i, j):
                row_re = jnp.where(lanes == e, count_ref[e], row_re)
                row_im = jnp.where(lanes == e, count_ref[e] if k == i else -count_ref[e], row_im)
        weight_re.append(row_re)
        weight_im.append(row_im)
    re_matrix = jnp.concatenate(one_hot + weight_re, axis=0)
    im_matrix = jnp.concatenate(hot_im + weight_im, axis=0)
    per_owner = 2 * cells * width // LANES
    for m in range(cells):
        for part, matrix in ((0, re_matrix), (1, im_matrix)):
            values = jnp.concatenate(
                [t[m, part * n : (part + 1) * n, :] for t, n in zip(tables, lengths)], axis=0
            )
            made = jnp.dot(
                matrix, values, precision=lax.Precision.HIGHEST, preferred_element_type=jnp.float32
            )
            sums_ref[part * 4 : part * 4 + 4, m * width : (m + 1) * width] = made[owners:]
            for t in range(width // LANES):
                piece = made[:owners, t * LANES : (t + 1) * LANES]
                start = (part * cells + m) * (width // LANES) + t
                slots_ref[pl.ds(start, owners, stride=per_owner), :] = piece


def selected(slot, sign, count, tables, owners):
    cells, _, width = tables[0].shape
    full = lambda a: pl.BlockSpec(a.shape, lambda: (0,) * len(a.shape))
    smem = pl.BlockSpec(memory_space=pltpu.SMEM)
    shape = (owners * 2 * cells * width // LANES, LANES)
    return pl.pallas_call(
        select_kernel,
        out_shape=[
            jax.ShapeDtypeStruct(shape, jnp.float32),
            jax.ShapeDtypeStruct((8, cells * width), jnp.float32),
        ],
        in_specs=[smem, smem, smem] + [full(a) for a in tables],
        out_specs=[pl.BlockSpec(shape, lambda: (0, 0)), pl.BlockSpec((8, cells * width), lambda: (0, 0))],
        compiler_params=pltpu.CompilerParams(vmem_limit_bytes=32 * 2**20),
    )(slot, sign, count, *tables)


def table_kernel(arrived_ref, out_ref):
    _, owners, cell_count = out_ref.shape
    tiles = cell_count // LANES
    for part in range(2):
        for t in range(tiles):
            out_ref[part, :, t * LANES : (t + 1) * LANES] = arrived_ref[
                pl.ds(part * tiles + t, owners, stride=2 * tiles), :
            ]


def as_table(arrived, owners, cell_count):
    return pl.pallas_call(
        table_kernel,
        out_shape=jax.ShapeDtypeStruct((2, owners, cell_count), jnp.float32),
        compiler_params=pltpu.CompilerParams(vmem_limit_bytes=32 * 2**20),
    )(arrived)


def shifted(value, axis, steps):
    count = lax.axis_size(axis)
    first, last = (max(0, -steps), min(count, count - steps))
    return lax.ppermute(value, axis, [(source, source + steps) for source in range(first, last)])


def on_device(images, date_pairs, assignment):
    owners = lax.axis_size("date")
    myself = lax.axis_index("date")
    local_dates = images.shape[1]
    columns = images.shape[3]
    below = shifted(images[:, local_dates - 2 :], "date", 1)
    above = shifted(images[:, :2], "date", -1)
    look_matrix = (
        jnp.arange(2 * COLUMNS)[:, None] // RLOOK == jnp.arange(LANES)[None, :]
    ).astype(jnp.bfloat16)

    anchor = myself * local_dates - 2
    first = date_pairs[:, 0] - anchor
    second = date_pairs[:, 1] - anchor
    low_date = jnp.minimum(first, second)
    high_date = jnp.maximum(first, second)
    known = jnp.array(KNOWN, jnp.int32)
    is_edge = (low_date[:, None] == known[None, :, 0]) & (high_date[:, None] == known[None, :, 1])
    count = jnp.sum(is_edge, axis=0).astype(jnp.float32)
    edge = jnp.sum(jnp.where(is_edge, jnp.arange(len(KNOWN))[None, :], 0), axis=1)
    mine = date_pairs[:, 0] // local_dates == myself
    matches = (assignment[None, :] // owners == jnp.arange(owners)[:, None]) & mine[None, :]
    present = jnp.any(matches, axis=1)
    slot = jnp.where(present, jnp.sum(jnp.where(matches, edge[None, :], 0), axis=1), -1)
    sign = jnp.sum(jnp.where(matches, jnp.where(first < second, 1.0, -1.0)[None, :], 0.0), axis=1)

    inner = looked_products(INNER, (2, 3, 4, 5), (images,), (2,), look_matrix)
    outer = looked_products(
        LOWER + UPPER, (0, 1, 6, 7), (below, images, above), (0, 2, 6), look_matrix
    )
    cells = inner.shape[0]
    inner_halo = (shifted(inner[cells - 1 :], "strip", 1), shifted(inner[:1], "strip", -1))
    outer_halo = (shifted(outer[cells - 1 :], "strip", 1), shifted(outer[:1], "strip", -1))
    own, low, up = coherences(inner, outer, inner_halo, outer_halo)
    from_below = shifted(up, "date", 1)
    from_above = shifted(low, "date", -1)
    slots, sums = selected(slot, sign, count, (own, low, up, from_below, from_above), owners)
    outgoing = slots.reshape(owners, slots.shape[0] // owners, LANES)
    arrived = lax.all_to_all(outgoing, "date", split_axis=0, concat_axis=0, tiled=True)
    cell_count = cells * (columns // RLOOK)
    coherence = as_table(arrived.reshape(slots.shape), owners, cell_count)
    return (coherence, sums.reshape(2, local_dates, cell_count))


def solution(mesh):
    return jax.shard_map(
        on_device,
        mesh=mesh,
        in_specs=(P(None, "date", "strip", None), P(), P()),
        out_specs=(P(None, "date", "strip"), P(None, "date", "strip")),
        check_vma=False,
    )
```

```python
import functools

import jax
import jax.numpy as jnp
from jax import lax
from jax.experimental import pallas as pl
from jax.experimental.pallas import tpu as pltpu
from jax.sharding import PartitionSpec as P

ALOOK = 5
RLOOK = 20
LANES = 128
TILE = 16
COLUMNS = 1280
FIXED = 32000.0
EPS_POWER = 1e-06
MIB = 2**20

INNER = ((2, 3), (2, 4), (2, 5), (3, 4), (3, 5), (4, 5))
LOWER = ((0, 4), (1, 4), (1, 5), (1, 2), (1, 3))
UPPER = ((2, 6), (3, 6), (3, 7), (4, 6), (4, 7))
OUTER = LOWER + UPPER
FROM_BELOW = tuple((i - 4, j - 4) for i, j in UPPER)
FROM_ABOVE = tuple((i + 4, j + 4) for i, j in LOWER)
KNOWN = INNER + OUTER + FROM_BELOW + FROM_ABOVE
INNER_POWERS = (2, 3, 4, 5)
OUTER_POWERS = (0, 1, 6, 7)


def products_kernel(edges, powers, places, groups, *refs):
    look_ref, out_ref, planes_ref, acc_ref = refs[-4:]
    width = planes_ref.shape[1]
    total = 2 * len(edges) + len(powers)
    rows = planes_ref.shape[0] // total
    step = pl.program_id(0)
    used = sorted({k for e in edges for k in e} | set(powers))

    def form(index, _):
        lane = pl.ds(pl.multiple_of(index * LANES, LANES), LANES)
        for tile in range(rows // TILE):
            pixel = {}
            for k in used:
                source, date, row = places[k][tile]
                pixel[k] = tuple(
                    refs[source][c, date, row : row + TILE, lane].astype(jnp.float32)
                    for c in (0, 1)
                )
            results = []
            for i, j in edges:
                results.append(pixel[i][0] * pixel[j][0] + pixel[i][1] * pixel[j][1])
            for i, j in edges:
                results.append(pixel[i][1] * pixel[j][0] - pixel[i][0] * pixel[j][1])
            for k in powers:
                results.append(pixel[k][0] * pixel[k][0] + pixel[k][1] * pixel[k][1])
            for p, value in enumerate(results):
                first = p * rows + tile * TILE
                planes_ref[first : first + TILE, lane] = value.astype(jnp.bfloat16)
        return 0

    lax.fori_loop(0, width // LANES, form, 0)
    part = jnp.dot(planes_ref[...], look_ref[...], preferred_element_type=jnp.float32)

    @pl.when(step % 2 == 0)
    def _():
        acc_ref[...] = part

    @pl.when(step % 2 == 1)
    def _():
        acc_ref[...] += part
        for m, (first, last) in enumerate(groups):
            for p in range(0, total, 8):
                size = min(8, total - p)
                value = acc_ref[pl.ds(p * rows + first, size, stride=rows), :]
                for row in range(first + 1, last):
                    value += acc_ref[pl.ds(p * rows + row, size, stride=rows), :]
                out_ref[m, p : p + size, :] = value


def looked_products(edges, powers, sources, places, groups, rows, columns, look_matrix):
    total = 2 * len(edges) + len(powers)

    def spec(block, index, offset):
        return pl.BlockSpec(block + (COLUMNS,), lambda i: index + (i + offset // COLUMNS,))

    return pl.pallas_call(
        functools.partial(products_kernel, edges, powers, places, groups),
        out_shape=jax.ShapeDtypeStruct((len(groups), total, columns // RLOOK), jnp.float32),
        grid=(columns // COLUMNS,),
        in_specs=[spec(*s[1:]) for s in sources]
        + [pl.BlockSpec((COLUMNS, LANES), lambda i: (i % 2, 0))],
        out_specs=pl.BlockSpec((len(groups), total, LANES), lambda i: (0, 0, i // 2)),
        scratch_shapes=[
            pltpu.VMEM((total * rows, COLUMNS), jnp.bfloat16),
            pltpu.VMEM((total * rows, LANES), jnp.float32),
        ],
        compiler_params=pltpu.CompilerParams(vmem_limit_bytes=48 * MIB),
    )(*[s[0] for s in sources], look_matrix)


def pack_kernel(parts, *refs):
    outs = refs[-2:]
    for n, (out, _, row) in enumerate(parts):
        outs[out][:, :, row : row + TILE, :] = refs[n][...]


def packed_rows(images, tiles):
    _, local_dates, _, columns = images.shape
    last = local_dates // 2 - 1
    parts = [(out, t, n * TILE) for out in range(2) for n, t in enumerate(tiles)]
    return pl.pallas_call(
        functools.partial(pack_kernel, parts),
        out_shape=[jax.ShapeDtypeStruct((2, 2, len(tiles) * TILE, columns), images.dtype)] * 2,
        grid=(columns // COLUMNS,),
        in_specs=[
            pl.BlockSpec((2, 2, TILE, COLUMNS), lambda i, d=last * (1 - out), t=t: (0, d, t, i))
            for out, t, _ in parts
        ],
        out_specs=[pl.BlockSpec((2, 2, len(tiles) * TILE, COLUMNS), lambda i: (0, 0, 0, i))] * 2,
        compiler_params=pltpu.CompilerParams(vmem_limit_bytes=32 * MIB),
    )(*[images] * len(parts))


def coherence_kernel(layout, *refs):
    inner_ref, first_ref, second_ref, before_ref, after_ref = refs[:5]
    outs = refs[5:]
    cells, n_first, width = inner_ref.shape
    n_in, n_out = len(INNER), len(OUTER)
    halves = width // LANES
    block = 2 * cells * halves

    def inner_at(m):
        if m < 0:
            return before_ref[0, :n_first]
        if m >= cells:
            return after_ref[0, :n_first]
        return inner_ref[m]

    def outer_at(m):
        if m < 0:
            return before_ref[0, n_first:]
        if m >= cells:
            return after_ref[0, n_first:]
        return sum(ref[n] for ref, n in zip((first_ref, second_ref), layout[m]) if n is not None)

    inners = [inner_at(m) for m in range(-1, cells + 1)]
    outers = [outer_at(m) for m in range(-1, cells + 1)]
    for m in range(cells):
        inner = inners[m] + 2.0 * inners[m + 1] + inners[m + 2]
        outer = outers[m] + 2.0 * outers[m + 1] + outers[m + 2]
        power = {}
        for n, k in enumerate(INNER_POWERS):
            power[k] = inner[2 * n_in + n : 2 * n_in + n + 1]
        for n, k in enumerate(OUTER_POWERS):
            power[k] = outer[2 * n_out + n : 2 * n_out + n + 1]
        for out, values, edges, start, count in (
            (outs[0], inner, INNER, 0, n_in),
            (outs[1], outer, LOWER, 0, n_out),
            (outs[2], outer, UPPER, len(LOWER), n_out),
        ):
            size = len(edges)
            first = jnp.concatenate([power[i] for i, _ in edges], axis=0)
            second = jnp.concatenate([power[j] for _, j in edges], axis=0)
            scale = lax.rsqrt(first * second + EPS_POWER)
            for part in range(2):
                begin = start + part * count
                value = values[begin : begin + size] * scale
                for h in range(halves):
                    row = (part * cells + m) * halves + h
                    out[pl.ds(row, size, stride=block), :] = value[:, h * LANES : (h + 1) * LANES]


def coherences(layout, inner, first, second, before, after):
    cells, _, width = inner.shape
    block = 2 * cells * (width // LANES)
    return pl.pallas_call(
        functools.partial(coherence_kernel, layout),
        out_shape=[
            jax.ShapeDtypeStruct((len(e) * block, LANES), jnp.float32)
            for e in (INNER, LOWER, UPPER)
        ],
        compiler_params=pltpu.CompilerParams(vmem_limit_bytes=32 * MIB),
    )(inner, first, second, before, after)


def slots_kernel(slot_ref, sign_ref, *refs):
    out_ref, known_ref = refs[-2:]
    owners, block, _ = out_ref.shape
    start = 0
    for table in refs[:-2]:
        known_ref[start : start + table.shape[0], :] = table[...]
        start += table.shape[0]
    for o in range(owners):
        row = pl.multiple_of(slot_ref[o] * block, block)
        value = known_ref[pl.ds(row, block), :]
        half = block // 2
        scales = (jnp.abs(sign_ref[o]) * FIXED, sign_ref[o] * FIXED)
        for part in range(2):
            fixed = jnp.round(value[part * half : (part + 1) * half] * scales[part])
            out_ref[o, part * half : (part + 1) * half, :] = fixed.astype(jnp.int32).astype(jnp.int16)


def slots_of(slot, sign, tables, owners, block):
    smem = pl.BlockSpec(memory_space=pltpu.SMEM)
    vmem = pl.BlockSpec(memory_space=pltpu.VMEM)
    return pl.pallas_call(
        slots_kernel,
        out_shape=jax.ShapeDtypeStruct((owners, block, LANES), jnp.int16),
        in_specs=[smem, smem] + [vmem] * len(tables),
        scratch_shapes=[pltpu.VMEM((len(KNOWN) * block, LANES), jnp.float32)],
        compiler_params=pltpu.CompilerParams(vmem_limit_bytes=32 * MIB),
    )(slot, sign, *tables)


def sums_kernel(count_ref, *refs):
    out_ref, rows_ref = refs[-2:]
    parts, dates, cell_count = out_ref.shape
    tiles = cell_count // LANES
    tables = []
    for table in refs[:-2]:
        tables += [(table, n * parts * tiles) for n in range(table.shape[0] // (parts * tiles))]
    for part in range(parts):
        totals = [jnp.zeros((tiles, LANES), jnp.float32) for _ in range(dates)]
        for e, (table, row) in enumerate(tables):
            value = table[row + part * tiles : row + (part + 1) * tiles, :] * count_ref[e]
            for d, k in enumerate(INNER_POWERS):
                if k == KNOWN[e][0] or (k == KNOWN[e][1] and part == 0):
                    totals[d] = totals[d] + value
                elif k == KNOWN[e][1]:
                    totals[d] = totals[d] - value
        for d in range(dates):
            first = (part * dates + d) * tiles
            rows_ref[first : first + tiles, :] = totals[d]
    for part in range(parts):
        for t in range(tiles):
            out_ref[part, :, t * LANES : (t + 1) * LANES] = rows_ref[
                pl.ds(part * dates * tiles + t, dates, stride=tiles), :
            ]


def sums_of(count, tables, local_dates, cell_count):
    smem = pl.BlockSpec(memory_space=pltpu.SMEM)
    vmem = pl.BlockSpec(memory_space=pltpu.VMEM)
    return pl.pallas_call(
        sums_kernel,
        out_shape=jax.ShapeDtypeStruct((2, local_dates, cell_count), jnp.float32),
        in_specs=[smem] + [vmem] * len(tables),
        scratch_shapes=[pltpu.VMEM((2 * local_dates * cell_count // LANES, LANES), jnp.float32)],
        compiler_params=pltpu.CompilerParams(vmem_limit_bytes=32 * MIB),
    )(count, *tables)


def table_kernel(arrived_ref, out_ref, rows_ref):
    parts, owners, cell_count = out_ref.shape
    tiles = cell_count // LANES
    for o in range(owners):
        rows_ref[o * parts * tiles : (o + 1) * parts * tiles, :] = arrived_ref[o].astype(
            jnp.int32
        ).astype(jnp.float32) * (1.0 / FIXED)
    for part in range(parts):
        for t in range(tiles):
            out_ref[part, :, t * LANES : (t + 1) * LANES] = rows_ref[
                pl.ds(part * tiles + t, owners, stride=parts * tiles), :
            ]


def as_table(arrived, cell_count):
    owners, block, _ = arrived.shape
    return pl.pallas_call(
        table_kernel,
        out_shape=jax.ShapeDtypeStruct((2, owners, cell_count), jnp.float32),
        scratch_shapes=[pltpu.VMEM((owners * block, LANES), jnp.float32)],
        compiler_params=pltpu.CompilerParams(vmem_limit_bytes=32 * MIB),
    )(arrived)


def shifted(value, axis, steps):
    count = lax.axis_size(axis)
    first, last = (max(0, -steps), min(count, count - steps))
    return lax.ppermute(value, axis, [(source, source + steps) for source in range(first, last)])


def pair_tables(date_pairs, assignment, myself, owners, local_dates):
    anchor = myself * local_dates - 2
    first = date_pairs[:, 0] - anchor
    second = date_pairs[:, 1] - anchor
    low_date = jnp.minimum(first, second)
    high_date = jnp.maximum(first, second)
    known = jnp.array(KNOWN, jnp.int32)
    is_edge = (low_date[:, None] == known[None, :, 0]) & (high_date[:, None] == known[None, :, 1])
    count = jnp.sum(is_edge, axis=0).astype(jnp.float32)
    edge = jnp.sum(jnp.where(is_edge, jnp.arange(len(KNOWN))[None, :], 0), axis=1)
    mine = date_pairs[:, 0] // local_dates == myself
    matches = (assignment[None, :] // owners == jnp.arange(owners)[:, None]) & mine[None, :]
    slot = jnp.sum(jnp.where(matches, edge[None, :], 0), axis=1)
    sign = jnp.sum(jnp.where(matches, jnp.where(first < second, 1.0, -1.0)[None, :], 0.0), axis=1)
    return slot, sign, count


def row_groups(tiles, cells):
    held = [t * TILE + r for t in tiles for r in range(TILE)]
    groups, owners = [], []
    for m in range(cells):
        local = [n for n, row in enumerate(held) if row // ALOOK == m]
        if local:
            groups.append((local[0], local[-1] + 1))
            owners.append(m)
    return groups, owners


def on_device(images, date_pairs, assignment):
    owners = lax.axis_size("date")
    myself = lax.axis_index("date")
    _, local_dates, rows, columns = images.shape
    cells = rows // ALOOK
    cell_count = cells * (columns // RLOOK)
    block = 2 * cell_count // LANES
    pieces = ((0,) + tuple(range(3, rows // TILE)), (1, 2))

    arrived = []
    for tiles in pieces:
        to_above, to_below = packed_rows(images, tiles)
        arrived.append((shifted(to_above, "date", 1), shifted(to_below, "date", -1)))

    look_matrix = (
        jnp.arange(2 * COLUMNS)[:, None] // RLOOK == jnp.arange(LANES)[None, :]
    ).astype(jnp.bfloat16)
    slot, sign, count = pair_tables(date_pairs, assignment, myself, owners, local_dates)

    own_places = {
        2 + d: [(0, d, t * TILE) for t in range(rows // TILE)] for d in range(local_dates)
    }
    inner = looked_products(
        INNER,
        INNER_POWERS,
        [(images, (2, local_dates, rows), (0, 0, 0), 0)],
        own_places,
        row_groups(range(rows // TILE), cells)[0],
        rows,
        columns,
        look_matrix,
    )
    layout = [[None, None] for _ in range(cells)]
    outer = []
    for piece, (tiles, (below, above)) in enumerate(zip(pieces, arrived)):
        size = len(tiles)
        sources = [
            (below, (2, 2, size * TILE), (0, 0, 0), 0),
            (above, (2, 2, size * TILE), (0, 0, 0), 0),
        ] + [(images, (2, local_dates, TILE), (0, 0, t), 0) for t in tiles]
        places = {d: [(0, d, t * TILE) for t in range(size)] for d in range(2)}
        places |= {6 + d: [(1, d, t * TILE) for t in range(size)] for d in range(2)}
        places |= {2 + d: [(2 + t, d, 0) for t in range(size)] for d in range(local_dates)}
        groups, where = row_groups(tiles, cells)
        for n, m in enumerate(where):
            layout[m][piece] = n
        outer.append(
            looked_products(
                OUTER, OUTER_POWERS, sources, places, groups, size * TILE, columns, look_matrix
            )
        )
    before = shifted(jnp.concatenate([inner[cells - 1 :], outer[0][-1:]], axis=1), "strip", 1)
    after = shifted(jnp.concatenate([inner[:1], outer[0][:1]], axis=1), "strip", -1)
    own, low, up = coherences(layout, inner, *outer, before, after)
    tables = (own, low, up, shifted(up, "date", 1), shifted(low, "date", -1))
    outgoing = slots_of(slot, sign, tables, owners, block)
    table = lax.all_to_all(outgoing, "date", split_axis=0, concat_axis=0, tiled=True)
    sums = sums_of(count, tables, local_dates, cell_count)
    return (as_table(table, cell_count), sums)


def solution(mesh):
    return jax.shard_map(
        on_device,
        mesh=mesh,
        in_specs=(P(None, "date", "strip", None), P(), P()),
        out_specs=(P(None, "date", "strip"), P(None, "date", "strip")),
        check_vma=False,
    )
```

```python
import functools

import jax
import jax.numpy as jnp
from jax import lax
from jax.experimental import pallas as pl
from jax.experimental.pallas import tpu as pltpu
from jax.sharding import PartitionSpec as P

ALOOK = 5
RLOOK = 20
LANES = 128
TILE = 16
COLUMNS = 1280
CHUNK = 256
FIXED = 32000.0
EPS_POWER = 1e-06
MIB = 2**20

INNER = ((2, 3), (2, 4), (2, 5), (3, 4), (3, 5), (4, 5))
LOWER = ((0, 4), (1, 4), (1, 5), (1, 2), (1, 3))
UPPER = ((2, 6), (3, 6), (3, 7), (4, 6), (4, 7))
OUTER = LOWER + UPPER
FROM_BELOW = tuple((i - 4, j - 4) for i, j in UPPER)
FROM_ABOVE = tuple((i + 4, j + 4) for i, j in LOWER)
KNOWN = INNER + OUTER + FROM_BELOW + FROM_ABOVE
INNER_POWERS = (2, 3, 4, 5)
OUTER_POWERS = (0, 1, 6, 7)


def products_kernel(edges, powers, places, groups, *refs):
    odd_device = refs[0][0] == 1
    out_ref, look_ref, even_ref, odd_ref, acc_ref = refs[-5:]
    total = 2 * len(edges) + len(powers)
    rows = acc_ref.shape[0] // total
    step = pl.program_id(0)
    used = sorted({k for e in edges for k in e} | set(powers))
    buffers = (even_ref, odd_ref)

    @pl.when(step == 0)
    def _():
        column = lax.broadcasted_iota(jnp.int32, look_ref.shape, 0)
        begin = lax.broadcasted_iota(jnp.int32, look_ref.shape, 1) * RLOOK
        inside = (column >= begin) & (column < begin + RLOOK)
        look_ref[...] = inside.astype(jnp.float32).astype(jnp.bfloat16)

    def form(chunk):
        for part in range(CHUNK // LANES):
            lane = slice(chunk * CHUNK + part * LANES, chunk * CHUNK + (part + 1) * LANES)
            out_lane = slice(part * LANES, (part + 1) * LANES)
            for tile in range(rows // TILE):
                pixel = {}
                for k in used:
                    sources, date, row = places[k][tile]
                    pixel[k] = []
                    for c in (0, 1):
                        found = [refs[1 + s][c, date, row : row + TILE, lane] for s in sources]
                        if len(found) == 2:
                            found = [jnp.where(odd_device, found[1], found[0])]
                        pixel[k].append(found[0].astype(jnp.float32))
                results = []
                for i, j in edges:
                    results.append(pixel[i][0] * pixel[j][0] + pixel[i][1] * pixel[j][1])
                for i, j in edges:
                    results.append(pixel[i][1] * pixel[j][0] - pixel[i][0] * pixel[j][1])
                for k in powers:
                    results.append(pixel[k][0] * pixel[k][0] + pixel[k][1] * pixel[k][1])
                for p, value in enumerate(results):
                    first = p * rows + tile * TILE
                    buffers[chunk % 2][first : first + TILE, out_lane] = value.astype(jnp.bfloat16)

    def add_looks(chunk):
        row = pl.multiple_of(step % 2 * COLUMNS + chunk * CHUNK, CHUNK)
        part = jnp.dot(
            buffers[chunk % 2][...],
            look_ref[pl.ds(row, CHUNK), :],
            preferred_element_type=jnp.float32,
        )
        if chunk == 0:
            acc_ref[...] = part + jnp.where(step % 2 == 1, acc_ref[...], 0.0)
        else:
            acc_ref[...] += part

    chunks = COLUMNS // CHUNK
    form(0)
    for chunk in range(chunks):
        if chunk + 1 < chunks:
            form(chunk + 1)
        add_looks(chunk)

    @pl.when(step % 2 == 1)
    def _():
        for m, (first, last) in enumerate(groups):
            for p in range(0, total, 8):
                size = min(8, total - p)
                value = acc_ref[pl.ds(p * rows + first, size, stride=rows), :]
                for row in range(first + 1, last):
                    value += acc_ref[pl.ds(p * rows + row, size, stride=rows), :]
                out_ref[m, p : p + size, :] = value


def looked_products(odd, edges, powers, sources, places, groups, rows, columns):
    total = 2 * len(edges) + len(powers)

    def spec(block, index):
        return pl.BlockSpec(block + (COLUMNS,), lambda i: index + (i,))

    return pl.pallas_call(
        functools.partial(products_kernel, edges, powers, places, groups),
        out_shape=jax.ShapeDtypeStruct((len(groups), total, columns // RLOOK), jnp.float32),
        grid=(columns // COLUMNS,),
        in_specs=[pl.BlockSpec(memory_space=pltpu.SMEM)] + [spec(*s[1:]) for s in sources],
        out_specs=pl.BlockSpec((len(groups), total, LANES), lambda i: (0, 0, i // 2)),
        scratch_shapes=[
            pltpu.VMEM((2 * COLUMNS, LANES), jnp.bfloat16),
            pltpu.VMEM((total * rows, CHUNK), jnp.bfloat16),
            pltpu.VMEM((total * rows, CHUNK), jnp.bfloat16),
            pltpu.VMEM((total * rows, LANES), jnp.float32),
        ],
        compiler_params=pltpu.CompilerParams(vmem_limit_bytes=48 * MIB),
    )(odd, *[s[0] for s in sources])


def pack_kernel(runs, odd_ref, images_ref, across_ref, beside_ref, held_ref, in_sems, out_sems):
    first = (2 * odd_ref[0], 2 - 2 * odd_ref[0])
    loads, stores = [], []
    for n, out in enumerate((across_ref, beside_ref)):
        for c in range(2):
            for row, target, size in runs:
                held = held_ref.at[n, c, :, target : target + size, :]
                loads.append(
                    pltpu.make_async_copy(
                        images_ref.at[c, pl.ds(first[n], 2), row : row + size, :],
                        held,
                        in_sems.at[len(loads)],
                    )
                )
                stores.append(
                    pltpu.make_async_copy(
                        held, out.at[c, :, target : target + size, :], out_sems.at[len(stores)]
                    )
                )
    for load in loads:
        load.start()
    for load, store in zip(loads, stores):
        load.wait()
        store.start()
    for store in stores:
        store.wait()


def packed_rows(odd, images, tiles, limit):
    columns = images.shape[3]
    runs = []
    for n, t in enumerate(tiles):
        if runs and runs[-1][0] + runs[-1][2] == t * TILE:
            row, target, size = runs.pop()
            runs.append((row, target, size + TILE))
        else:
            runs.append((t * TILE, n * TILE, TILE))
    return pl.pallas_call(
        functools.partial(pack_kernel, runs),
        out_shape=[jax.ShapeDtypeStruct((2, 2, len(tiles) * TILE, columns), images.dtype)] * 2,
        in_specs=[pl.BlockSpec(memory_space=pltpu.SMEM), pl.BlockSpec(memory_space=pl.ANY)],
        out_specs=[pl.BlockSpec(memory_space=pl.ANY)] * 2,
        scratch_shapes=[
            pltpu.VMEM((2, 2, 2, len(tiles) * TILE, columns), images.dtype),
            pltpu.SemaphoreType.DMA((4 * len(runs),)),
            pltpu.SemaphoreType.DMA((4 * len(runs),)),
        ],
        compiler_params=pltpu.CompilerParams(vmem_limit_bytes=limit * MIB),
    )(odd, images)


def coherence_kernel(layout, *refs):
    odd_ref, inner_ref, first_ref, second_ref, before_ref, after_ref = refs[:6]
    outs = refs[6:9]
    across_ref, beside_ref = refs[9:]
    cells, n_first, width = inner_ref.shape
    n_in, n_out = len(INNER), len(OUTER)
    halves = width // LANES
    block = 2 * cells * halves

    def inner_at(m):
        if m < 0:
            return before_ref[0, :n_first]
        if m >= cells:
            return after_ref[0, :n_first]
        return inner_ref[m]

    def outer_at(m):
        if m < 0:
            return before_ref[0, n_first:]
        if m >= cells:
            return after_ref[0, n_first:]
        return sum(ref[n] for ref, n in zip((first_ref, second_ref), layout[m]) if n is not None)

    inners = [inner_at(m) for m in range(-1, cells + 1)]
    outers = [outer_at(m) for m in range(-1, cells + 1)]
    for m in range(cells):
        inner = inners[m] + 2.0 * inners[m + 1] + inners[m + 2]
        outer = outers[m] + 2.0 * outers[m + 1] + outers[m + 2]
        power = {}
        for n, k in enumerate(INNER_POWERS):
            power[k] = inner[2 * n_in + n : 2 * n_in + n + 1]
        for n, k in enumerate(OUTER_POWERS):
            power[k] = outer[2 * n_out + n : 2 * n_out + n + 1]
        for out, values, edges, start, count in (
            (outs[0], inner, INNER, 0, n_in),
            (outs[1], outer, LOWER, 0, n_out),
            (outs[2], outer, UPPER, len(LOWER), n_out),
        ):
            size = len(edges)
            first = jnp.concatenate([power[i] for i, _ in edges], axis=0)
            second = jnp.concatenate([power[j] for _, j in edges], axis=0)
            scale = lax.rsqrt(first * second + EPS_POWER)
            for part in range(2):
                begin = start + part * count
                value = values[begin : begin + size] * scale
                for h in range(halves):
                    row = (part * cells + m) * halves + h
                    out[pl.ds(row, size, stride=block), :] = value[:, h * LANES : (h + 1) * LANES]

    @pl.when(odd_ref[0] == 0)
    def _():
        across_ref[...] = outs[1][...]
        beside_ref[...] = outs[2][...]

    @pl.when(odd_ref[0] == 1)
    def _():
        across_ref[...] = outs[2][...]
        beside_ref[...] = outs[1][...]


def coherences(layout, odd, inner, first, second, before, after):
    cells, _, width = inner.shape
    block = 2 * cells * (width // LANES)
    vmem = pl.BlockSpec(memory_space=pltpu.VMEM)
    return pl.pallas_call(
        functools.partial(coherence_kernel, layout),
        out_shape=[
            jax.ShapeDtypeStruct((len(e) * block, LANES), jnp.float32)
            for e in (INNER, LOWER, UPPER, LOWER, UPPER)
        ],
        in_specs=[pl.BlockSpec(memory_space=pltpu.SMEM)] + [vmem] * 5,
        compiler_params=pltpu.CompilerParams(vmem_limit_bytes=32 * MIB),
    )(odd, inner, first, second, before, after)


def slots_kernel(odd_ref, slot_ref, sign_ref, *refs):
    out_ref, known_ref = refs[-2:]
    owners, block, _ = out_ref.shape
    start = 0
    own, (across, beside) = refs[:-4], refs[-4:-2]
    for table in own:
        known_ref[start : start + table.shape[0], :] = table[...]
        start += table.shape[0]
    size = across.shape[0]
    across_at = pl.multiple_of(start + odd_ref[0] * size, 8)
    beside_at = pl.multiple_of(start + (1 - odd_ref[0]) * size, 8)
    known_ref[pl.ds(across_at, size), :] = across[...]
    known_ref[pl.ds(beside_at, size), :] = beside[...]
    for o in range(owners):
        row = pl.multiple_of(slot_ref[o] * block, block)
        value = known_ref[pl.ds(row, block), :]
        half = block // 2
        scales = (jnp.abs(sign_ref[o]) * FIXED, sign_ref[o] * FIXED)
        for part in range(2):
            fixed = jnp.round(value[part * half : (part + 1) * half] * scales[part])
            out_ref[o, part * half : (part + 1) * half, :] = fixed.astype(jnp.int32).astype(jnp.int16)


def slots_of(odd, slot, sign, tables, owners, block):
    smem = pl.BlockSpec(memory_space=pltpu.SMEM)
    vmem = pl.BlockSpec(memory_space=pltpu.VMEM)
    return pl.pallas_call(
        slots_kernel,
        out_shape=[
            jax.ShapeDtypeStruct((owners, block, LANES), jnp.int16),
            jax.ShapeDtypeStruct((len(KNOWN) * block, LANES), jnp.float32),
        ],
        in_specs=[smem, smem, smem] + [vmem] * len(tables),
        compiler_params=pltpu.CompilerParams(vmem_limit_bytes=32 * MIB),
    )(odd, slot, sign, *tables)


def sums_kernel(count_ref, known_ref, out_ref, rows_ref):
    parts, dates, cell_count = out_ref.shape
    tiles = cell_count // LANES
    for part in range(parts):
        totals = [jnp.zeros((tiles, LANES), jnp.float32) for _ in range(dates)]
        for e, (low, high) in enumerate(KNOWN):
            row = (e * parts + part) * tiles
            value = known_ref[row : row + tiles, :] * count_ref[e]
            for d, k in enumerate(INNER_POWERS):
                if k == low or (k == high and part == 0):
                    totals[d] = totals[d] + value
                elif k == high:
                    totals[d] = totals[d] - value
        for d in range(dates):
            first = (part * dates + d) * tiles
            rows_ref[first : first + tiles, :] = totals[d]
    for part in range(parts):
        for t in range(tiles):
            out_ref[part, :, t * LANES : (t + 1) * LANES] = rows_ref[
                pl.ds(part * dates * tiles + t, dates, stride=tiles), :
            ]


def sums_of(count, known, local_dates, cell_count):
    smem = pl.BlockSpec(memory_space=pltpu.SMEM)
    vmem = pl.BlockSpec(memory_space=pltpu.VMEM)
    return pl.pallas_call(
        sums_kernel,
        out_shape=jax.ShapeDtypeStruct((2, local_dates, cell_count), jnp.float32),
        in_specs=[smem, vmem],
        scratch_shapes=[pltpu.VMEM((2 * local_dates * cell_count // LANES, LANES), jnp.float32)],
        compiler_params=pltpu.CompilerParams(vmem_limit_bytes=32 * MIB),
    )(count, known)


def table_kernel(arrived_ref, out_ref, rows_ref):
    parts, owners, cell_count = out_ref.shape
    tiles = cell_count // LANES
    for o in range(owners):
        rows_ref[o * parts * tiles : (o + 1) * parts * tiles, :] = arrived_ref[o].astype(
            jnp.int32
        ).astype(jnp.float32) * (1.0 / FIXED)
    for part in range(parts):
        for t in range(tiles):
            out_ref[part, :, t * LANES : (t + 1) * LANES] = rows_ref[
                pl.ds(part * tiles + t, owners, stride=parts * tiles), :
            ]


def as_table(arrived, cell_count):
    owners, block, _ = arrived.shape
    return pl.pallas_call(
        table_kernel,
        out_shape=jax.ShapeDtypeStruct((2, owners, cell_count), jnp.float32),
        scratch_shapes=[pltpu.VMEM((owners * block, LANES), jnp.float32)],
        compiler_params=pltpu.CompilerParams(vmem_limit_bytes=32 * MIB),
    )(arrived)


def shifted(value, axis, steps):
    count = lax.axis_size(axis)
    first, last = (max(0, -steps), min(count, count - steps))
    return lax.ppermute(value, axis, [(source, source + steps) for source in range(first, last)])


def swapped(across, beside):
    count = lax.axis_size("date")
    over = [(i, i + 1) for i in range(1, count - 1, 2)]
    within = [(i, i + 1) for i in range(0, count, 2)]
    return tuple(
        lax.ppermute(value, "date", pairs + [(b, a) for a, b in pairs])
        for value, pairs in ((across, over), (beside, within))
    )


def pair_tables(date_pairs, assignment, myself, owners, local_dates):
    anchor = myself * local_dates - 2
    first = date_pairs[:, 0] - anchor
    second = date_pairs[:, 1] - anchor
    low_date = jnp.minimum(first, second)
    high_date = jnp.maximum(first, second)
    known = jnp.array(KNOWN, jnp.int32)
    is_edge = (low_date[:, None] == known[None, :, 0]) & (high_date[:, None] == known[None, :, 1])
    count = jnp.sum(is_edge, axis=0).astype(jnp.float32)
    edge = jnp.sum(jnp.where(is_edge, jnp.arange(len(KNOWN))[None, :], 0), axis=1)
    mine = date_pairs[:, 0] // local_dates == myself
    matches = (assignment[None, :] // owners == jnp.arange(owners)[:, None]) & mine[None, :]
    slot = jnp.sum(jnp.where(matches, edge[None, :], 0), axis=1)
    sign = jnp.sum(jnp.where(matches, jnp.where(first < second, 1.0, -1.0)[None, :], 0.0), axis=1)
    return slot, sign, count


def row_groups(tiles, cells):
    held = [t * TILE + r for t in tiles for r in range(TILE)]
    groups, owners = [], []
    for m in range(cells):
        local = [n for n, row in enumerate(held) if row // ALOOK == m]
        if local:
            groups.append((local[0], local[-1] + 1))
            owners.append(m)
    return groups, owners


def on_device(images, date_pairs, assignment):
    owners = lax.axis_size("date")
    myself = lax.axis_index("date")
    _, local_dates, rows, columns = images.shape
    cells = rows // ALOOK
    cell_count = cells * (columns // RLOOK)
    pieces = ((0,) + tuple(range(3, rows // TILE)), (1, 2))

    odd = (myself % 2).astype(jnp.int32)[None]

    def sent(source, tiles, limit):
        return swapped(*packed_rows(odd, source, tiles, limit))

    slot, sign, count = pair_tables(date_pairs, assignment, myself, owners, local_dates)
    arrived = [sent(images, pieces[0], 60)]
    own_places = {
        2 + d: [((0,), d, t * TILE) for t in range(rows // TILE)] for d in range(local_dates)
    }
    inner = looked_products(
        odd,
        INNER,
        INNER_POWERS,
        [(images, (2, local_dates, rows), (0, 0, 0))],
        own_places,
        row_groups(range(rows // TILE), cells)[0],
        rows,
        columns,
    )
    later, inner = lax.optimization_barrier((images, inner))
    arrived.append(sent(later, pieces[1], 32))
    layout = [[None, None] for _ in range(cells)]
    outer = []
    for piece, (tiles, (across, beside)) in enumerate(zip(pieces, arrived)):
        size = len(tiles)
        block = (2, 2, size * TILE)
        sources = [(across, block, (0, 0, 0)), (beside, block, (0, 0, 0))]
        sources += [(images, (2, local_dates, TILE), (0, 0, t)) for t in tiles]
        places = {d: [((0, 1), d, t * TILE) for t in range(size)] for d in range(2)}
        places |= {6 + d: [((1, 0), d, t * TILE) for t in range(size)] for d in range(2)}
        places |= {2 + d: [((2 + t,), d, 0) for t in range(size)] for d in range(local_dates)}
        groups, where = row_groups(tiles, cells)
        for n, m in enumerate(where):
            layout[m][piece] = n
        outer.append(
            looked_products(
                odd, OUTER, OUTER_POWERS, sources, places, groups, size * TILE, columns
            )
        )
    before = shifted(jnp.concatenate([inner[cells - 1 :], outer[0][-1:]], axis=1), "strip", 1)
    after = shifted(jnp.concatenate([inner[:1], outer[0][:1]], axis=1), "strip", -1)
    own, low, up, *sides = coherences(layout, odd, inner, *outer, before, after)
    tables = (own, low, up, *swapped(*sides))
    outgoing, known = slots_of(odd, slot, sign, tables, owners, 2 * cell_count // LANES)
    table = lax.all_to_all(outgoing, "date", split_axis=0, concat_axis=0, tiled=True)
    sums = sums_of(count, known, local_dates, cell_count)
    return (as_table(table, cell_count), sums)


def solution(mesh):
    return jax.shard_map(
        on_device,
        mesh=mesh,
        in_specs=(P(None, "date", "strip", None), P(), P()),
        out_specs=(P(None, "date", "strip"), P(None, "date", "strip")),
        check_vma=False,
    )
```

```python
import functools

import jax
import jax.numpy as jnp
from jax import lax
from jax.experimental import pallas as pl
from jax.experimental.pallas import tpu as pltpu
from jax.sharding import PartitionSpec as P

ALOOK = 5
RLOOK = 20
LANES = 128
TILE = 16
COLUMNS = 1280
CHUNK = 256
FIXED = 32000.0
EPS_POWER = 1e-06
MIB = 2**20

INNER = ((2, 3), (2, 4), (2, 5), (3, 4), (3, 5), (4, 5))
SIDE = ((0, 4), (1, 4), (1, 5), (0, 2), (0, 3), (1, 2))
BACK = 4
RETURNED = tuple((3 - i, 3 - j) for i, j in SIDE[:BACK])
OWN_PLACES = (2, 3, 4, 5)
NEAR_PLACES = (0, 1)
KNOWN = tuple(
    (i, j, across)
    for edges, across in ((INNER, 0), (SIDE, 0), (SIDE, 1), (RETURNED, 1), (RETURNED, 0))
    for i, j in edges
)
FORMED = len(INNER) + 2 * len(SIDE)


def products_kernel(edges, powers, places, groups, *refs):
    flip = refs[0][0]
    out_ref, look_ref, even_ref, odd_ref, acc_ref = refs[-5:]
    total = 2 * len(edges) + len(powers)
    rows = acc_ref.shape[0] // total
    step = pl.program_id(0)
    used = sorted({k for e in edges for k in e} | set(powers))
    buffers = (even_ref, odd_ref)

    @pl.when(step == 0)
    def _():
        column = lax.broadcasted_iota(jnp.int32, look_ref.shape, 0)
        begin = lax.broadcasted_iota(jnp.int32, look_ref.shape, 1) * RLOOK
        inside = (column >= begin) & (column < begin + RLOOK)
        look_ref[...] = inside.astype(jnp.float32).astype(jnp.bfloat16)

    def form(chunk):
        for part in range(CHUNK // LANES):
            lane = slice(chunk * CHUNK + part * LANES, chunk * CHUNK + (part + 1) * LANES)
            out_lane = slice(part * LANES, (part + 1) * LANES)
            for tile in range(rows // TILE):
                pixel = {}
                for k in used:
                    source, date, row = places[k][tile]
                    ref = refs[1 + source]
                    date = date + flip * (ref.shape[1] - 1 - 2 * date)
                    pixel[k] = tuple(
                        ref[c, date, row : row + TILE, lane].astype(jnp.float32) for c in (0, 1)
                    )
                results = []
                for i, j in edges:
                    results.append(pixel[i][0] * pixel[j][0] + pixel[i][1] * pixel[j][1])
                for i, j in edges:
                    results.append(pixel[i][1] * pixel[j][0] - pixel[i][0] * pixel[j][1])
                for k in powers:
                    results.append(pixel[k][0] * pixel[k][0] + pixel[k][1] * pixel[k][1])
                for p, value in enumerate(results):
                    first = p * rows + tile * TILE
                    buffers[chunk % 2][first : first + TILE, out_lane] = value.astype(jnp.bfloat16)

    def add_looks(chunk):
        row = pl.multiple_of(step % 2 * COLUMNS + chunk * CHUNK, CHUNK)
        part = jnp.dot(
            buffers[chunk % 2][...],
            look_ref[pl.ds(row, CHUNK), :],
            preferred_element_type=jnp.float32,
        )
        if chunk == 0:
            acc_ref[...] = part + jnp.where(step % 2 == 1, acc_ref[...], 0.0)
        else:
            acc_ref[...] += part

    chunks = COLUMNS // CHUNK
    form(0)
    for chunk in range(chunks):
        if chunk + 1 < chunks:
            form(chunk + 1)
        add_looks(chunk)

    @pl.when(step % 2 == 1)
    def _():
        for m, (first, last) in enumerate(groups):
            for p in range(0, total, 8):
                size = min(8, total - p)
                value = acc_ref[pl.ds(p * rows + first, size, stride=rows), :]
                for row in range(first + 1, last):
                    value += acc_ref[pl.ds(p * rows + row, size, stride=rows), :]
                out_ref[m, p : p + size, :] = value


def looked_products(flip, edges, powers, sources, places, groups, rows, columns):
    total = 2 * len(edges) + len(powers)

    def spec(block, index):
        return pl.BlockSpec(block + (COLUMNS,), lambda i: index + (i,))

    return pl.pallas_call(
        functools.partial(products_kernel, edges, powers, places, groups),
        out_shape=jax.ShapeDtypeStruct((len(groups), total, columns // RLOOK), jnp.float32),
        grid=(columns // COLUMNS,),
        in_specs=[pl.BlockSpec(memory_space=pltpu.SMEM)] + [spec(*s[1:]) for s in sources],
        out_specs=pl.BlockSpec((len(groups), total, LANES), lambda i: (0, 0, i // 2)),
        scratch_shapes=[
            pltpu.VMEM((2 * COLUMNS, LANES), jnp.bfloat16),
            pltpu.VMEM((total * rows, CHUNK), jnp.bfloat16),
            pltpu.VMEM((total * rows, CHUNK), jnp.bfloat16),
            pltpu.VMEM((total * rows, LANES), jnp.float32),
        ],
        compiler_params=pltpu.CompilerParams(vmem_limit_bytes=48 * MIB),
    )(flip, *[s[0] for s in sources])


def pack_kernel(runs, flip_ref, images_ref, out_ref, held_ref, in_sems, out_sems):
    first = 2 * flip_ref[0]
    loads, stores = [], []
    for c in range(2):
        for row, target, size in runs:
            held = held_ref.at[c, :, target : target + size, :]
            loads.append(
                pltpu.make_async_copy(
                    images_ref.at[c, pl.ds(first, 2), row : row + size, :],
                    held,
                    in_sems.at[len(loads)],
                )
            )
            stores.append(
                pltpu.make_async_copy(
                    held, out_ref.at[c, :, target : target + size, :], out_sems.at[len(stores)]
                )
            )
    for load in loads:
        load.start()
    for load, store in zip(loads, stores):
        load.wait()
        store.start()
    for store in stores:
        store.wait()


def packed_rows(flip, images, runs, limit):
    columns = images.shape[3]
    rows = sum(size for _, _, size in runs)
    return pl.pallas_call(
        functools.partial(pack_kernel, runs),
        out_shape=jax.ShapeDtypeStruct((2, 2, rows, columns), images.dtype),
        in_specs=[pl.BlockSpec(memory_space=pltpu.SMEM), pl.BlockSpec(memory_space=pl.ANY)],
        out_specs=pl.BlockSpec(memory_space=pl.ANY),
        scratch_shapes=[
            pltpu.VMEM((2, 2, rows, columns), images.dtype),
            pltpu.SemaphoreType.DMA((2 * len(runs),)),
            pltpu.SemaphoreType.DMA((2 * len(runs),)),
        ],
        compiler_params=pltpu.CompilerParams(vmem_limit_bytes=limit * MIB),
    )(flip, images)


def coherence_kernel(layout, *refs):
    inner_ref, beside_ref, first_ref, second_ref, before_ref, after_ref = refs[:6]
    formed_ref, across_back_ref, beside_back_ref = refs[6:]
    cells, n_first, width = inner_ref.shape
    n_second = beside_ref.shape[1]
    halves = width // LANES
    block = 2 * cells * halves

    def padded(at, start, size):
        planes = slice(start, start + size)
        return (
            [before_ref[0, planes]] + [at(m) for m in range(cells)] + [after_ref[0, planes]]
        )

    def across_at(m):
        return sum(ref[n] for ref, n in zip((first_ref, second_ref), layout[m]) if n is not None)

    rows = (
        padded(lambda m: inner_ref[m], 0, n_first),
        padded(lambda m: beside_ref[m], n_first, n_second),
        padded(across_at, n_first + n_second, n_second),
    )
    for m in range(cells):
        inner, beside, across = (r[m] + 2.0 * r[m + 1] + r[m + 2] for r in rows)

        def power_of(smooth, edges, n):
            return smooth[2 * len(edges) + n : 2 * len(edges) + n + 1]

        beside_power = {k: power_of(beside, SIDE, n) for n, k in enumerate(NEAR_PLACES)}
        across_power = {k: power_of(across, SIDE, n) for n, k in enumerate(NEAR_PLACES)}
        for n, k in enumerate(OWN_PLACES):
            beside_power[k] = power_of(inner, INNER, n)
            across_power[7 - k] = beside_power[k]
        start = 0
        for values, edges, power, back_ref in (
            (inner, INNER, beside_power, None),
            (beside, SIDE, beside_power, beside_back_ref),
            (across, SIDE, across_power, across_back_ref),
        ):
            size = len(edges)
            first = jnp.concatenate([power[i] for i, _ in edges], axis=0)
            second = jnp.concatenate([power[j] for _, j in edges], axis=0)
            scale = lax.rsqrt(first * second + EPS_POWER)
            for part in range(2):
                value = values[part * size : (part + 1) * size] * scale
                for h in range(halves):
                    row = (part * cells + m) * halves + h
                    piece = value[:, h * LANES : (h + 1) * LANES]
                    formed_ref[pl.ds(start * block + row, size, stride=block), :] = piece
                    if back_ref is not None:
                        back_ref[pl.ds(row, BACK, stride=block), :] = piece[:BACK]
            start += size


def coherences(layout, inner, beside, first, second, before, after):
    cells, _, width = inner.shape
    block = 2 * cells * (width // LANES)
    return pl.pallas_call(
        functools.partial(coherence_kernel, layout),
        out_shape=[
            jax.ShapeDtypeStruct((n * block, LANES), jnp.float32) for n in (FORMED, BACK, BACK)
        ],
        compiler_params=pltpu.CompilerParams(vmem_limit_bytes=32 * MIB),
    )(inner, beside, first, second, before, after)


def slots_kernel(odd_ref, slot_ref, sign_ref, count_ref, *refs):
    out_ref, sums_ref, known_ref, rows_ref = refs[-4:]
    owners, block, _ = out_ref.shape
    start = 0
    for table in refs[:-4]:
        known_ref[start : start + table.shape[0], :] = table[...]
        start += table.shape[0]
    for o in range(owners):
        row = pl.multiple_of(slot_ref[o] * block, block)
        value = known_ref[pl.ds(row, block), :]
        half = block // 2
        scales = (jnp.abs(sign_ref[o]) * FIXED, sign_ref[o] * FIXED)
        for part in range(2):
            fixed = jnp.round(value[part * half : (part + 1) * half] * scales[part])
            out_ref[o, part * half : (part + 1) * half, :] = fixed.astype(jnp.int32).astype(jnp.int16)
    parts, dates, cell_count = sums_ref.shape
    tiles = cell_count // LANES
    for part in range(parts):
        totals = {k: jnp.zeros((tiles, LANES), jnp.float32) for k in OWN_PLACES}
        for e, (first, second, across) in enumerate(KNOWN):
            row = (e * parts + part) * tiles
            value = known_ref[row : row + tiles, :] * count_ref[e]
            for k in OWN_PLACES:
                place = k if across else 7 - k
                if place == first or (place == second and part == 0):
                    totals[k] = totals[k] + value
                elif place == second:
                    totals[k] = totals[k] - value
        for d, k in enumerate(OWN_PLACES):
            date = d + odd_ref[0] * (dates - 1 - 2 * d)
            first = pl.multiple_of((part * dates + date) * tiles, tiles)
            rows_ref[pl.ds(first, tiles), :] = totals[k]
    for part in range(parts):
        for t in range(tiles):
            sums_ref[part, :, t * LANES : (t + 1) * LANES] = rows_ref[
                pl.ds(part * dates * tiles + t, dates, stride=tiles), :
            ]


def slots_and_sums(odd, slot, sign, count, tables, owners, local_dates, cell_count):
    smem = pl.BlockSpec(memory_space=pltpu.SMEM)
    vmem = pl.BlockSpec(memory_space=pltpu.VMEM)
    block = 2 * cell_count // LANES
    return pl.pallas_call(
        slots_kernel,
        out_shape=[
            jax.ShapeDtypeStruct((owners, block, LANES), jnp.int16),
            jax.ShapeDtypeStruct((2, local_dates, cell_count), jnp.float32),
        ],
        in_specs=[smem] * 4 + [vmem] * len(tables),
        scratch_shapes=[
            pltpu.VMEM((len(KNOWN) * block, LANES), jnp.float32),
            pltpu.VMEM((local_dates * block, LANES), jnp.float32),
        ],
        compiler_params=pltpu.CompilerParams(vmem_limit_bytes=32 * MIB),
    )(odd, slot, sign, count, *tables)


def table_kernel(arrived_ref, out_ref, rows_ref):
    parts, owners, cell_count = out_ref.shape
    tiles = cell_count // LANES
    for o in range(owners):
        rows_ref[o * parts * tiles : (o + 1) * parts * tiles, :] = arrived_ref[o].astype(
            jnp.int32
        ).astype(jnp.float32) * (1.0 / FIXED)
    for part in range(parts):
        for t in range(tiles):
            out_ref[part, :, t * LANES : (t + 1) * LANES] = rows_ref[
                pl.ds(part * tiles + t, owners, stride=parts * tiles), :
            ]


def as_table(arrived, cell_count):
    owners, block, _ = arrived.shape
    return pl.pallas_call(
        table_kernel,
        out_shape=jax.ShapeDtypeStruct((2, owners, cell_count), jnp.float32),
        scratch_shapes=[pltpu.VMEM((owners * block, LANES), jnp.float32)],
        compiler_params=pltpu.CompilerParams(vmem_limit_bytes=32 * MIB),
    )(arrived)


def shifted(value, axis, steps):
    count = lax.axis_size(axis)
    first, last = (max(0, -steps), min(count, count - steps))
    return lax.ppermute(value, axis, [(source, source + steps) for source in range(first, last)])


def swapped_across(value):
    pairs = [(i, i + 1) for i in range(1, lax.axis_size("date") - 1, 2)]
    return lax.ppermute(value, "date", pairs + [(b, a) for a, b in pairs])


def swapped_beside(value):
    pairs = [(i, i + 1) for i in range(0, lax.axis_size("date"), 2)]
    return lax.ppermute(value, "date", pairs + [(b, a) for a, b in pairs])


def pair_tables(date_pairs, assignment, myself, owners, local_dates):
    anchor = myself * local_dates - 2
    first = date_pairs[:, 0] - anchor
    second = date_pairs[:, 1] - anchor
    known = jnp.array(KNOWN, jnp.int32)
    flipped = (known[:, 2] == 1) == (myself % 2 == 1)
    known_first = jnp.where(flipped, 7 - known[:, 0], known[:, 0])[None, :]
    known_second = jnp.where(flipped, 7 - known[:, 1], known[:, 1])[None, :]
    first, second = first[:, None], second[:, None]
    forward = (first == known_first) & (second == known_second)
    backward = (first == known_second) & (second == known_first)
    is_edge = forward | backward
    count = jnp.sum(is_edge, axis=0).astype(jnp.float32)
    edge = jnp.sum(jnp.where(is_edge, jnp.arange(len(KNOWN))[None, :], 0), axis=1)
    way = jnp.sum(forward.astype(jnp.float32) - backward.astype(jnp.float32), axis=1)
    mine = date_pairs[:, 0] // local_dates == myself
    matches = (assignment[None, :] // owners == jnp.arange(owners)[:, None]) & mine[None, :]
    slot = jnp.sum(jnp.where(matches, edge[None, :], 0), axis=1)
    sign = jnp.sum(jnp.where(matches, way[None, :], 0.0), axis=1)
    return slot, sign, count


def row_groups(tiles, cells):
    held = [t * TILE + r for t in tiles for r in range(TILE)]
    groups, owners = [], []
    for m in range(cells):
        local = [n for n, row in enumerate(held) if row // ALOOK == m]
        if local:
            groups.append((local[0], local[-1] + 1))
            owners.append(m)
    return groups, owners


def on_device(images, date_pairs, assignment):
    owners = lax.axis_size("date")
    myself = lax.axis_index("date")
    _, local_dates, rows, columns = images.shape
    cells = rows // ALOOK
    cell_count = cells * (columns // RLOOK)
    tiles = rows // TILE
    pieces = ((0,) + tuple(range(3, tiles)), (1, 2))
    runs = (((0, 0, TILE), (3 * TILE, TILE, rows - 3 * TILE)), ((TILE, 0, 2 * TILE),))
    odd = (myself % 2).astype(jnp.int32)[None]
    even = 1 - odd

    beside = swapped_beside(images)
    across = [swapped_across(packed_rows(odd, images, runs[0], 60))]
    slot, sign, count = pair_tables(date_pairs, assignment, myself, owners, local_dates)

    all_groups = row_groups(range(tiles), cells)[0]
    own_source = (images, (2, local_dates, rows), (0, 0, 0))
    own_places = {
        2 + d: [(0, d, t * TILE) for t in range(tiles)] for d in range(local_dates)
    }
    inner = looked_products(
        even, INNER, OWN_PLACES, [own_source], own_places, all_groups, rows, columns
    )
    later, inner = lax.optimization_barrier((images, inner))
    across.append(swapped_across(packed_rows(odd, later, runs[1], 60)))

    side_places = own_places | {
        d: [(1, local_dates - 2 + d, t * TILE) for t in range(tiles)] for d in range(2)
    }
    beside_looked = looked_products(
        even,
        SIDE,
        NEAR_PLACES,
        [own_source, (beside, (2, local_dates, rows), (0, 0, 0))],
        side_places,
        all_groups,
        rows,
        columns,
    )
    later, beside_looked = lax.optimization_barrier((images, beside_looked))
    layout = [[None, None] for _ in range(cells)]
    across_looked = []
    for n, (piece, arrived) in enumerate(zip(pieces, across)):
        size = len(piece)
        sources = [(arrived, (2, 2, size * TILE), (0, 0, 0))]
        sources += [(later, (2, local_dates, TILE), (0, 0, t)) for t in piece]
        places = {d: [(0, d, t * TILE) for t in range(size)] for d in range(2)}
        places |= {2 + d: [(1 + t, d, 0) for t in range(size)] for d in range(local_dates)}
        groups, where = row_groups(piece, cells)
        for g, m in enumerate(where):
            layout[m][n] = g
        across_looked.append(
            looked_products(odd, SIDE, NEAR_PLACES, sources, places, groups, size * TILE, columns)
        )

    def edge_cells(cut):
        return jnp.concatenate([inner[cut], beside_looked[cut], across_looked[0][cut]], axis=1)

    before = shifted(edge_cells(slice(-1, None)), "strip", 1)
    after = shifted(edge_cells(slice(0, 1)), "strip", -1)
    formed, across_back, beside_back = coherences(
        layout, inner, beside_looked, *across_looked, before, after
    )
    tables = (formed, swapped_across(across_back), swapped_beside(beside_back))
    outgoing, sums = slots_and_sums(
        odd, slot, sign, count, tables, owners, local_dates, cell_count
    )
    table = lax.all_to_all(outgoing, "date", split_axis=0, concat_axis=0, tiled=True)
    return (as_table(table, cell_count), sums)


def solution(mesh):
    return jax.shard_map(
        on_device,
        mesh=mesh,
        in_specs=(P(None, "date", "strip", None), P(), P()),
        out_specs=(P(None, "date", "strip"), P(None, "date", "strip")),
        check_vma=False,
    )
```

```python
import functools

import jax
import jax.numpy as jnp
from jax import lax
from jax.experimental import pallas as pl
from jax.experimental.pallas import tpu as pltpu
from jax.sharding import PartitionSpec as P

ALOOK = 5
RLOOK = 20
LANES = 128
TILE = 16
COLUMNS = 1280
FIXED = 32000.0
EPS_POWER = 1e-06
MIB = 2**20

INNER = ((2, 3), (2, 4), (2, 5), (3, 4), (3, 5), (4, 5))
SIDE = ((0, 4), (1, 4), (1, 5), (0, 2), (0, 3), (1, 2))
BACK = 4
RETURNED = tuple((3 - i, 3 - j) for i, j in SIDE[:BACK])
OWN_PLACES = (2, 3, 4, 5)
NEAR_PLACES = (0, 1)
KNOWN = tuple(
    (i, j, across)
    for edges, across in ((INNER, 0), (SIDE, 0), (SIDE, 1), (RETURNED, 1), (RETURNED, 0))
    for i, j in edges
)
FORMED = len(INNER) + 2 * len(SIDE)


def products_kernel(edges, powers, places, groups, *refs):
    flip = refs[0][0]
    out_ref, look_ref, acc_ref = refs[-3:]
    total = 2 * len(edges) + len(powers)
    tiles = acc_ref.shape[0] // (total * TILE)
    step = pl.program_id(0)
    used = sorted({k for e in edges for k in e} | set(powers))

    @pl.when(step == 0)
    def _():
        column = lax.broadcasted_iota(jnp.int32, look_ref.shape, 0)
        begin = lax.broadcasted_iota(jnp.int32, look_ref.shape, 1) * RLOOK
        inside = (column >= begin) & (column < begin + RLOOK)
        look_ref[...] = inside.astype(jnp.float32).astype(jnp.bfloat16)

    def planes(tile, start):
        pixel = {}
        for k in used:
            source, date, row = places[k][tile]
            ref = refs[1 + source]
            date = date + flip * (ref.shape[1] - 1 - 2 * date)
            pixel[k] = tuple(
                ref[c, date, row : row + TILE, start : start + LANES].astype(jnp.float32)
                for c in (0, 1)
            )
        results = []
        for i, j in edges:
            results.append(pixel[i][0] * pixel[j][0] + pixel[i][1] * pixel[j][1])
        for i, j in edges:
            results.append(pixel[i][1] * pixel[j][0] - pixel[i][0] * pixel[j][1])
        for k in powers:
            results.append(pixel[k][0] * pixel[k][0] + pixel[k][1] * pixel[k][1])
        return jnp.concatenate([r.astype(jnp.bfloat16) for r in results], axis=0)

    look = look_ref[pl.ds(pl.multiple_of(step % 2 * COLUMNS, COLUMNS), COLUMNS), :]
    for tile in range(tiles):
        formed = jnp.concatenate([planes(tile, s) for s in range(0, COLUMNS, LANES)], axis=1)
        part = jnp.dot(formed, look, preferred_element_type=jnp.float32)
        span = slice(tile * total * TILE, (tile + 1) * total * TILE)
        acc_ref[span, :] = part + jnp.where(step % 2 == 1, acc_ref[span, :], 0.0)

    @pl.when(step % 2 == 1)
    def _():
        for m, (first, last) in enumerate(groups):
            for p in range(0, total, 8):
                size = min(8, total - p)

                def plane_rows(row):
                    start = (row // TILE * total + p) * TILE + row % TILE
                    return acc_ref[pl.ds(start, size, stride=TILE), :]

                value = plane_rows(first)
                for row in range(first + 1, last):
                    value += plane_rows(row)
                out_ref[m, p : p + size, :] = value


def looked_products(flip, edges, powers, sources, places, groups, rows, columns):
    total = 2 * len(edges) + len(powers)

    def spec(block, index):
        return pl.BlockSpec(block + (COLUMNS,), lambda i: index + (i,))

    return pl.pallas_call(
        functools.partial(products_kernel, edges, powers, places, groups),
        out_shape=jax.ShapeDtypeStruct((len(groups), total, columns // RLOOK), jnp.float32),
        grid=(columns // COLUMNS,),
        in_specs=[pl.BlockSpec(memory_space=pltpu.SMEM)] + [spec(*s[1:]) for s in sources],
        out_specs=pl.BlockSpec((len(groups), total, LANES), lambda i: (0, 0, i // 2)),
        scratch_shapes=[
            pltpu.VMEM((2 * COLUMNS, LANES), jnp.bfloat16),
            pltpu.VMEM((total * rows, LANES), jnp.float32),
        ],
        compiler_params=pltpu.CompilerParams(vmem_limit_bytes=48 * MIB),
    )(flip, *[s[0] for s in sources])


def pack_kernel(runs, flip_ref, images_ref, out_ref, held_ref, in_sems, out_sems):
    first = 2 * flip_ref[0]
    loads, stores = [], []
    for c in range(2):
        for row, target, size in runs:
            held = held_ref.at[c, :, target : target + size, :]
            loads.append(
                pltpu.make_async_copy(
                    images_ref.at[c, pl.ds(first, 2), row : row + size, :],
                    held,
                    in_sems.at[len(loads)],
                )
            )
            stores.append(
                pltpu.make_async_copy(
                    held, out_ref.at[c, :, target : target + size, :], out_sems.at[len(stores)]
                )
            )
    for load in loads:
        load.start()
    for load, store in zip(loads, stores):
        load.wait()
        store.start()
    for store in stores:
        store.wait()


def packed_rows(flip, images, runs, limit):
    columns = images.shape[3]
    rows = sum(size for _, _, size in runs)
    return pl.pallas_call(
        functools.partial(pack_kernel, runs),
        out_shape=jax.ShapeDtypeStruct((2, 2, rows, columns), images.dtype),
        in_specs=[pl.BlockSpec(memory_space=pltpu.SMEM), pl.BlockSpec(memory_space=pl.ANY)],
        out_specs=pl.BlockSpec(memory_space=pl.ANY),
        scratch_shapes=[
            pltpu.VMEM((2, 2, rows, columns), images.dtype),
            pltpu.SemaphoreType.DMA((2 * len(runs),)),
            pltpu.SemaphoreType.DMA((2 * len(runs),)),
        ],
        compiler_params=pltpu.CompilerParams(vmem_limit_bytes=limit * MIB),
    )(flip, images)


def coherence_kernel(layout, *refs):
    inner_ref, beside_ref, first_ref, second_ref, before_ref, after_ref = refs[:6]
    formed_ref, across_back_ref, beside_back_ref = refs[6:]
    cells, n_first, width = inner_ref.shape
    n_second = beside_ref.shape[1]
    halves = width // LANES
    block = 2 * cells * halves

    def padded(at, start, size):
        planes = slice(start, start + size)
        return (
            [before_ref[0, planes]] + [at(m) for m in range(cells)] + [after_ref[0, planes]]
        )

    def across_at(m):
        return sum(ref[n] for ref, n in zip((first_ref, second_ref), layout[m]) if n is not None)

    rows = (
        padded(lambda m: inner_ref[m], 0, n_first),
        padded(lambda m: beside_ref[m], n_first, n_second),
        padded(across_at, n_first + n_second, n_second),
    )
    for m in range(cells):
        inner, beside, across = (r[m] + 2.0 * r[m + 1] + r[m + 2] for r in rows)

        def power_of(smooth, edges, n):
            return smooth[2 * len(edges) + n : 2 * len(edges) + n + 1]

        beside_power = {k: power_of(beside, SIDE, n) for n, k in enumerate(NEAR_PLACES)}
        across_power = {k: power_of(across, SIDE, n) for n, k in enumerate(NEAR_PLACES)}
        for n, k in enumerate(OWN_PLACES):
            beside_power[k] = power_of(inner, INNER, n)
            across_power[7 - k] = beside_power[k]
        start = 0
        for values, edges, power in (
            (inner, INNER, beside_power),
            (beside, SIDE, beside_power),
            (across, SIDE, across_power),
        ):
            size = len(edges)
            first = jnp.concatenate([power[i] for i, _ in edges], axis=0)
            second = jnp.concatenate([power[j] for _, j in edges], axis=0)
            scale = lax.rsqrt(first * second + EPS_POWER)
            for part in range(2):
                value = values[part * size : (part + 1) * size] * scale
                for h in range(halves):
                    row = (part * cells + m) * halves + h
                    piece = value[:, h * LANES : (h + 1) * LANES]
                    formed_ref[pl.ds(start * block + row, size, stride=block), :] = piece
            start += size
    size = BACK * block
    for back_ref, first in (
        (beside_back_ref, len(INNER) * block),
        (across_back_ref, (len(INNER) + len(SIDE)) * block),
    ):
        fixed = jnp.round(formed_ref[first : first + size, :] * FIXED)
        back_ref[...] = fixed.astype(jnp.int32).astype(jnp.int16)


def coherences(layout, inner, beside, first, second, before, after):
    cells, _, width = inner.shape
    block = 2 * cells * (width // LANES)
    return pl.pallas_call(
        functools.partial(coherence_kernel, layout),
        out_shape=[
            jax.ShapeDtypeStruct((n * block, LANES), dtype)
            for n, dtype in ((FORMED, jnp.float32), (BACK, jnp.int16), (BACK, jnp.int16))
        ],
        compiler_params=pltpu.CompilerParams(vmem_limit_bytes=32 * MIB),
    )(inner, beside, first, second, before, after)


def slots_kernel(odd_ref, slot_ref, sign_ref, count_ref, *refs):
    out_ref, sums_ref, known_ref, rows_ref = refs[-4:]
    owners, block, _ = out_ref.shape
    start = 0
    for table in refs[:-4]:
        value = table[...]
        if table.dtype == jnp.int16:
            value = value.astype(jnp.int32).astype(jnp.float32) * (1.0 / FIXED)
        known_ref[start : start + table.shape[0], :] = value
        start += table.shape[0]
    for o in range(owners):
        row = pl.multiple_of(slot_ref[o] * block, block)
        value = known_ref[pl.ds(row, block), :]
        half = block // 2
        scales = (jnp.abs(sign_ref[o]) * FIXED, sign_ref[o] * FIXED)
        for part in range(2):
            fixed = jnp.round(value[part * half : (part + 1) * half] * scales[part])
            out_ref[o, part * half : (part + 1) * half, :] = fixed.astype(jnp.int32).astype(jnp.int16)
    parts, dates, cell_count = sums_ref.shape
    tiles = cell_count // LANES
    for part in range(parts):
        totals = {k: jnp.zeros((tiles, LANES), jnp.float32) for k in OWN_PLACES}
        for e, (first, second, across) in enumerate(KNOWN):
            row = (e * parts + part) * tiles
            value = known_ref[row : row + tiles, :] * count_ref[e]
            for k in OWN_PLACES:
                place = k if across else 7 - k
                if place == first or (place == second and part == 0):
                    totals[k] = totals[k] + value
                elif place == second:
                    totals[k] = totals[k] - value
        for d, k in enumerate(OWN_PLACES):
            date = d + odd_ref[0] * (dates - 1 - 2 * d)
            first = pl.multiple_of((part * dates + date) * tiles, tiles)
            rows_ref[pl.ds(first, tiles), :] = totals[k]
    for part in range(parts):
        for t in range(tiles):
            sums_ref[part, :, t * LANES : (t + 1) * LANES] = rows_ref[
                pl.ds(part * dates * tiles + t, dates, stride=tiles), :
            ]


def slots_and_sums(odd, slot, sign, count, tables, owners, local_dates, cell_count):
    smem = pl.BlockSpec(memory_space=pltpu.SMEM)
    vmem = pl.BlockSpec(memory_space=pltpu.VMEM)
    block = 2 * cell_count // LANES
    return pl.pallas_call(
        slots_kernel,
        out_shape=[
            jax.ShapeDtypeStruct((owners, block, LANES), jnp.int16),
            jax.ShapeDtypeStruct((2, local_dates, cell_count), jnp.float32),
        ],
        in_specs=[smem] * 4 + [vmem] * len(tables),
        scratch_shapes=[
            pltpu.VMEM((len(KNOWN) * block, LANES), jnp.float32),
            pltpu.VMEM((local_dates * block, LANES), jnp.float32),
        ],
        compiler_params=pltpu.CompilerParams(vmem_limit_bytes=32 * MIB),
    )(odd, slot, sign, count, *tables)


def table_kernel(arrived_ref, out_ref, rows_ref):
    parts, owners, cell_count = out_ref.shape
    tiles = cell_count // LANES
    for o in range(owners):
        rows_ref[o * parts * tiles : (o + 1) * parts * tiles, :] = arrived_ref[o].astype(
            jnp.int32
        ).astype(jnp.float32) * (1.0 / FIXED)
    for part in range(parts):
        for t in range(tiles):
            out_ref[part, :, t * LANES : (t + 1) * LANES] = rows_ref[
                pl.ds(part * tiles + t, owners, stride=parts * tiles), :
            ]


def as_table(arrived, cell_count):
    owners, block, _ = arrived.shape
    return pl.pallas_call(
        table_kernel,
        out_shape=jax.ShapeDtypeStruct((2, owners, cell_count), jnp.float32),
        scratch_shapes=[pltpu.VMEM((owners * block, LANES), jnp.float32)],
        compiler_params=pltpu.CompilerParams(vmem_limit_bytes=32 * MIB),
    )(arrived)


def shifted(value, axis, steps):
    count = lax.axis_size(axis)
    first, last = (max(0, -steps), min(count, count - steps))
    return lax.ppermute(value, axis, [(source, source + steps) for source in range(first, last)])


def swapped_across(value):
    pairs = [(i, i + 1) for i in range(1, lax.axis_size("date") - 1, 2)]
    return lax.ppermute(value, "date", pairs + [(b, a) for a, b in pairs])


def swapped_beside(value):
    pairs = [(i, i + 1) for i in range(0, lax.axis_size("date"), 2)]
    return lax.ppermute(value, "date", pairs + [(b, a) for a, b in pairs])


def pair_tables(date_pairs, assignment, myself, owners, local_dates):
    anchor = myself * local_dates - 2
    first = date_pairs[:, 0] - anchor
    second = date_pairs[:, 1] - anchor
    known = jnp.array(KNOWN, jnp.int32)
    flipped = (known[:, 2] == 1) == (myself % 2 == 1)
    known_first = jnp.where(flipped, 7 - known[:, 0], known[:, 0])[None, :]
    known_second = jnp.where(flipped, 7 - known[:, 1], known[:, 1])[None, :]
    first, second = first[:, None], second[:, None]
    forward = (first == known_first) & (second == known_second)
    backward = (first == known_second) & (second == known_first)
    is_edge = forward | backward
    count = jnp.sum(is_edge, axis=0).astype(jnp.float32)
    edge = jnp.sum(jnp.where(is_edge, jnp.arange(len(KNOWN))[None, :], 0), axis=1)
    way = jnp.sum(forward.astype(jnp.float32) - backward.astype(jnp.float32), axis=1)
    mine = date_pairs[:, 0] // local_dates == myself
    matches = (assignment[None, :] // owners == jnp.arange(owners)[:, None]) & mine[None, :]
    slot = jnp.sum(jnp.where(matches, edge[None, :], 0), axis=1)
    sign = jnp.sum(jnp.where(matches, way[None, :], 0.0), axis=1)
    return slot, sign, count


def row_groups(tiles, cells):
    held = [t * TILE + r for t in tiles for r in range(TILE)]
    groups, owners = [], []
    for m in range(cells):
        local = [n for n, row in enumerate(held) if row // ALOOK == m]
        if local:
            groups.append((local[0], local[-1] + 1))
            owners.append(m)
    return groups, owners


def on_device(images, date_pairs, assignment):
    owners = lax.axis_size("date")
    myself = lax.axis_index("date")
    _, local_dates, rows, columns = images.shape
    cells = rows // ALOOK
    cell_count = cells * (columns // RLOOK)
    tiles = rows // TILE
    pieces = ((0,) + tuple(range(3, tiles)), (1, 2))
    runs = (((0, 0, TILE), (3 * TILE, TILE, rows - 3 * TILE)), ((TILE, 0, 2 * TILE),))
    odd = (myself % 2).astype(jnp.int32)[None]
    even = 1 - odd

    packed = packed_rows(odd, images, runs[0], 60)
    later, packed = lax.optimization_barrier((images, packed))
    across = [swapped_across(packed)]
    beside = swapped_beside(later)
    slot, sign, count = pair_tables(date_pairs, assignment, myself, owners, local_dates)

    all_groups = row_groups(range(tiles), cells)[0]
    own_source = (images, (2, local_dates, rows), (0, 0, 0))
    own_places = {
        2 + d: [(0, d, t * TILE) for t in range(tiles)] for d in range(local_dates)
    }
    inner = looked_products(
        even, INNER, OWN_PLACES, [own_source], own_places, all_groups, rows, columns
    )
    later, inner = lax.optimization_barrier((images, inner))
    across.append(swapped_across(packed_rows(odd, later, runs[1], 60)))

    side_places = own_places | {
        d: [(1, local_dates - 2 + d, t * TILE) for t in range(tiles)] for d in range(2)
    }
    beside_looked = looked_products(
        even,
        SIDE,
        NEAR_PLACES,
        [own_source, (beside, (2, local_dates, rows), (0, 0, 0))],
        side_places,
        all_groups,
        rows,
        columns,
    )
    later, beside_looked = lax.optimization_barrier((images, beside_looked))
    layout = [[None, None] for _ in range(cells)]
    across_looked = []
    for n, (piece, arrived) in enumerate(zip(pieces, across)):
        size = len(piece)
        sources = [(arrived, (2, 2, size * TILE), (0, 0, 0))]
        sources += [(later, (2, local_dates, TILE), (0, 0, t)) for t in piece]
        places = {d: [(0, d, t * TILE) for t in range(size)] for d in range(2)}
        places |= {2 + d: [(1 + t, d, 0) for t in range(size)] for d in range(local_dates)}
        groups, where = row_groups(piece, cells)
        for g, m in enumerate(where):
            layout[m][n] = g
        across_looked.append(
            looked_products(odd, SIDE, NEAR_PLACES, sources, places, groups, size * TILE, columns)
        )

    def edge_cells(cut):
        return jnp.concatenate([inner[cut], beside_looked[cut], across_looked[0][cut]], axis=1)

    before = shifted(edge_cells(slice(-1, None)), "strip", 1)
    after = shifted(edge_cells(slice(0, 1)), "strip", -1)
    formed, across_back, beside_back = coherences(
        layout, inner, beside_looked, *across_looked, before, after
    )
    tables = (formed, swapped_across(across_back), swapped_beside(beside_back))
    outgoing, sums = slots_and_sums(
        odd, slot, sign, count, tables, owners, local_dates, cell_count
    )
    table = lax.all_to_all(outgoing, "date", split_axis=0, concat_axis=0, tiled=True)
    return (as_table(table, cell_count), sums)


def solution(mesh):
    return jax.shard_map(
        on_device,
        mesh=mesh,
        in_specs=(P(None, "date", "strip", None), P(), P()),
        out_specs=(P(None, "date", "strip"), P(None, "date", "strip")),
        check_vma=False,
    )
```

```python
import functools

import jax
import jax.numpy as jnp
from jax import lax
from jax.experimental import pallas as pl
from jax.experimental.pallas import tpu as pltpu
from jax.sharding import PartitionSpec as P

ALOOK = 5
RLOOK = 20
LANES = 128
TILE = 16
COLUMNS = 1280
FIXED = 32000.0
EPS_POWER = 1e-06
MIB = 2**20

INNER = ((2, 3), (2, 4), (2, 5), (3, 4), (3, 5), (4, 5))
SIDE = ((0, 4), (1, 4), (1, 5), (0, 2), (0, 3), (1, 2))
BACK = 4
RETURNED = tuple((3 - i, 3 - j) for i, j in SIDE[:BACK])
OWN_PLACES = (2, 3, 4, 5)
NEAR_PLACES = (0, 1)
KNOWN = tuple(
    (i, j, across)
    for edges, across in ((INNER, 0), (SIDE, 0), (SIDE, 1), (RETURNED, 1), (RETURNED, 0))
    for i, j in edges
)
FORMED = len(INNER) + 2 * len(SIDE)


def products_kernel(edges, powers, places, groups, *refs):
    flip = refs[0][0]
    out_ref, look_ref, acc_ref = refs[-3:]
    total = 2 * len(edges) + len(powers)
    tiles = acc_ref.shape[0] // (total * TILE)
    step = pl.program_id(0)
    used = sorted({k for e in edges for k in e} | set(powers))

    @pl.when(step == 0)
    def _():
        column = lax.broadcasted_iota(jnp.int32, look_ref.shape, 0)
        begin = lax.broadcasted_iota(jnp.int32, look_ref.shape, 1) * RLOOK
        inside = (column >= begin) & (column < begin + RLOOK)
        look_ref[...] = inside.astype(jnp.float32).astype(jnp.bfloat16)

    def planes(tile, start):
        pixel = {}
        for k in used:
            source, date, row = places[k][tile]
            ref = refs[1 + source]
            date = date + flip * (ref.shape[1] - 1 - 2 * date)
            pixel[k] = tuple(
                ref[c, date, row : row + TILE, start : start + LANES].astype(jnp.float32)
                for c in (0, 1)
            )
        results = []
        for i, j in edges:
            results.append(pixel[i][0] * pixel[j][0] + pixel[i][1] * pixel[j][1])
        for i, j in edges:
            results.append(pixel[i][1] * pixel[j][0] - pixel[i][0] * pixel[j][1])
        for k in powers:
            results.append(pixel[k][0] * pixel[k][0] + pixel[k][1] * pixel[k][1])
        return jnp.concatenate([r.astype(jnp.bfloat16) for r in results], axis=0)

    look = look_ref[pl.ds(pl.multiple_of(step % 2 * COLUMNS, COLUMNS), COLUMNS), :]
    for tile in range(tiles):
        formed = jnp.concatenate([planes(tile, s) for s in range(0, COLUMNS, LANES)], axis=1)
        part = jnp.dot(formed, look, preferred_element_type=jnp.float32)
        span = slice(tile * total * TILE, (tile + 1) * total * TILE)
        acc_ref[span, :] = part + jnp.where(step % 2 == 1, acc_ref[span, :], 0.0)

    @pl.when(step % 2 == 1)
    def _():
        for m, (first, last) in enumerate(groups):
            for p in range(0, total, 8):
                size = min(8, total - p)

                def plane_rows(row):
                    start = (row // TILE * total + p) * TILE + row % TILE
                    return acc_ref[pl.ds(start, size, stride=TILE), :]

                value = plane_rows(first)
                for row in range(first + 1, last):
                    value += plane_rows(row)
                out_ref[m, p : p + size, :] = value


def looked_products(flip, edges, powers, sources, places, groups, rows, columns):
    total = 2 * len(edges) + len(powers)

    def spec(block, index):
        return pl.BlockSpec(block + (COLUMNS,), lambda i: index + (i,))

    return pl.pallas_call(
        functools.partial(products_kernel, edges, powers, places, groups),
        out_shape=jax.ShapeDtypeStruct((len(groups), total, columns // RLOOK), jnp.float32),
        grid=(columns // COLUMNS,),
        in_specs=[pl.BlockSpec(memory_space=pltpu.SMEM)] + [spec(*s[1:]) for s in sources],
        out_specs=pl.BlockSpec((len(groups), total, LANES), lambda i: (0, 0, i // 2)),
        scratch_shapes=[
            pltpu.VMEM((2 * COLUMNS, LANES), jnp.bfloat16),
            pltpu.VMEM((total * rows, LANES), jnp.float32),
        ],
        compiler_params=pltpu.CompilerParams(vmem_limit_bytes=48 * MIB),
    )(flip, *[s[0] for s in sources])


def pack_kernel(runs, flip_ref, images_ref, out_ref, semaphores):
    first = 2 * flip_ref[0]
    copies = []
    for c in range(2):
        for row, target, size in runs:
            copies.append(
                pltpu.make_async_copy(
                    images_ref.at[c, pl.ds(first, 2), row : row + size, :],
                    out_ref.at[c, :, target : target + size, :],
                    semaphores.at[len(copies)],
                )
            )
    for copy in copies:
        copy.start()
    for copy in copies:
        copy.wait()


def packed_rows(flip, images, runs, limit):
    columns = images.shape[3]
    rows = sum(size for _, _, size in runs)
    return pl.pallas_call(
        functools.partial(pack_kernel, runs),
        out_shape=jax.ShapeDtypeStruct((2, 2, rows, columns), images.dtype),
        in_specs=[pl.BlockSpec(memory_space=pltpu.SMEM), pl.BlockSpec(memory_space=pl.ANY)],
        out_specs=pl.BlockSpec(memory_space=pltpu.VMEM),
        scratch_shapes=[pltpu.SemaphoreType.DMA((2 * len(runs),))],
        compiler_params=pltpu.CompilerParams(vmem_limit_bytes=limit * MIB),
    )(flip, images)


def coherence_kernel(layout, *refs):
    inner_ref, beside_ref, first_ref, second_ref, before_ref, after_ref = refs[:6]
    formed_ref, across_back_ref, beside_back_ref = refs[6:]
    cells, n_first, width = inner_ref.shape
    n_second = beside_ref.shape[1]
    halves = width // LANES
    block = 2 * cells * halves

    def padded(at, start, size):
        planes = slice(start, start + size)
        return (
            [before_ref[0, planes]] + [at(m) for m in range(cells)] + [after_ref[0, planes]]
        )

    def across_at(m):
        return sum(ref[n] for ref, n in zip((first_ref, second_ref), layout[m]) if n is not None)

    rows = (
        padded(lambda m: inner_ref[m], 0, n_first),
        padded(lambda m: beside_ref[m], n_first, n_second),
        padded(across_at, n_first + n_second, n_second),
    )
    for m in range(cells):
        inner, beside, across = (r[m] + 2.0 * r[m + 1] + r[m + 2] for r in rows)

        def power_of(smooth, edges, n):
            return smooth[2 * len(edges) + n : 2 * len(edges) + n + 1]

        beside_power = {k: power_of(beside, SIDE, n) for n, k in enumerate(NEAR_PLACES)}
        across_power = {k: power_of(across, SIDE, n) for n, k in enumerate(NEAR_PLACES)}
        for n, k in enumerate(OWN_PLACES):
            beside_power[k] = power_of(inner, INNER, n)
            across_power[7 - k] = beside_power[k]
        start = 0
        for values, edges, power in (
            (inner, INNER, beside_power),
            (beside, SIDE, beside_power),
            (across, SIDE, across_power),
        ):
            size = len(edges)
            first = jnp.concatenate([power[i] for i, _ in edges], axis=0)
            second = jnp.concatenate([power[j] for _, j in edges], axis=0)
            scale = lax.rsqrt(first * second + EPS_POWER)
            for part in range(2):
                value = values[part * size : (part + 1) * size] * scale
                for h in range(halves):
                    row = (part * cells + m) * halves + h
                    piece = value[:, h * LANES : (h + 1) * LANES]
                    formed_ref[pl.ds(start * block + row, size, stride=block), :] = piece
            start += size
    size = BACK * block
    for back_ref, first in (
        (beside_back_ref, len(INNER) * block),
        (across_back_ref, (len(INNER) + len(SIDE)) * block),
    ):
        fixed = jnp.round(formed_ref[first : first + size, :] * FIXED)
        back_ref[...] = fixed.astype(jnp.int32).astype(jnp.int16)


def coherences(layout, inner, beside, first, second, before, after):
    cells, _, width = inner.shape
    block = 2 * cells * (width // LANES)
    return pl.pallas_call(
        functools.partial(coherence_kernel, layout),
        out_shape=[
            jax.ShapeDtypeStruct((n * block, LANES), dtype)
            for n, dtype in ((FORMED, jnp.float32), (BACK, jnp.int16), (BACK, jnp.int16))
        ],
        compiler_params=pltpu.CompilerParams(vmem_limit_bytes=32 * MIB),
    )(inner, beside, first, second, before, after)


def slots_kernel(scalar_ref, *refs):
    out_ref, sums_ref, known_ref, rows_ref = refs[-4:]
    owners, block, _ = out_ref.shape
    odd = scalar_ref[0]
    start = 0
    for table in refs[:-4]:
        value = table[...]
        if table.dtype == jnp.int16:
            value = value.astype(jnp.int32).astype(jnp.float32) * (1.0 / FIXED)
        known_ref[start : start + table.shape[0], :] = value
        start += table.shape[0]
    for o in range(owners):
        row = pl.multiple_of(scalar_ref[1 + o] * block, block)
        value = known_ref[pl.ds(row, block), :]
        half = block // 2
        sign = scalar_ref[1 + owners + o].astype(jnp.float32)
        scales = (jnp.abs(sign) * FIXED, sign * FIXED)
        for part in range(2):
            fixed = jnp.round(value[part * half : (part + 1) * half] * scales[part])
            out_ref[o, part * half : (part + 1) * half, :] = fixed.astype(jnp.int32).astype(jnp.int16)
    parts, dates, cell_count = sums_ref.shape
    tiles = cell_count // LANES
    for part in range(parts):
        totals = {k: jnp.zeros((tiles, LANES), jnp.float32) for k in OWN_PLACES}
        for e, (first, second, across) in enumerate(KNOWN):
            row = (e * parts + part) * tiles
            count = scalar_ref[1 + 2 * owners + e].astype(jnp.float32)
            value = known_ref[row : row + tiles, :] * count
            for k in OWN_PLACES:
                place = k if across else 7 - k
                if place == first or (place == second and part == 0):
                    totals[k] = totals[k] + value
                elif place == second:
                    totals[k] = totals[k] - value
        for d, k in enumerate(OWN_PLACES):
            date = d + odd * (dates - 1 - 2 * d)
            first = pl.multiple_of((part * dates + date) * tiles, tiles)
            rows_ref[pl.ds(first, tiles), :] = totals[k]
    for part in range(parts):
        for t in range(tiles):
            sums_ref[part, :, t * LANES : (t + 1) * LANES] = rows_ref[
                pl.ds(part * dates * tiles + t, dates, stride=tiles), :
            ]


def slots_and_sums(scalars, tables, owners, local_dates, cell_count):
    smem = pl.BlockSpec(memory_space=pltpu.SMEM)
    vmem = pl.BlockSpec(memory_space=pltpu.VMEM)
    block = 2 * cell_count // LANES
    return pl.pallas_call(
        slots_kernel,
        out_shape=[
            jax.ShapeDtypeStruct((owners, block, LANES), jnp.int16),
            jax.ShapeDtypeStruct((2, local_dates, cell_count), jnp.float32),
        ],
        in_specs=[smem] + [vmem] * len(tables),
        scratch_shapes=[
            pltpu.VMEM((len(KNOWN) * block, LANES), jnp.float32),
            pltpu.VMEM((local_dates * block, LANES), jnp.float32),
        ],
        compiler_params=pltpu.CompilerParams(vmem_limit_bytes=32 * MIB),
    )(scalars, *tables)


def table_kernel(arrived_ref, out_ref, rows_ref):
    parts, owners, cell_count = out_ref.shape
    tiles = cell_count // LANES
    for o in range(owners):
        rows_ref[o * parts * tiles : (o + 1) * parts * tiles, :] = arrived_ref[o].astype(
            jnp.int32
        ).astype(jnp.float32) * (1.0 / FIXED)
    for part in range(parts):
        for t in range(tiles):
            out_ref[part, :, t * LANES : (t + 1) * LANES] = rows_ref[
                pl.ds(part * tiles + t, owners, stride=parts * tiles), :
            ]


def as_table(arrived, cell_count):
    owners, block, _ = arrived.shape
    return pl.pallas_call(
        table_kernel,
        out_shape=jax.ShapeDtypeStruct((2, owners, cell_count), jnp.float32),
        scratch_shapes=[pltpu.VMEM((owners * block, LANES), jnp.float32)],
        compiler_params=pltpu.CompilerParams(vmem_limit_bytes=32 * MIB),
    )(arrived)


def shifted(value, axis, steps):
    count = lax.axis_size(axis)
    first, last = (max(0, -steps), min(count, count - steps))
    return lax.ppermute(value, axis, [(source, source + steps) for source in range(first, last)])


def swapped_across(value):
    pairs = [(i, i + 1) for i in range(1, lax.axis_size("date") - 1, 2)]
    return lax.ppermute(value, "date", pairs + [(b, a) for a, b in pairs])


def swapped_beside(value):
    pairs = [(i, i + 1) for i in range(0, lax.axis_size("date"), 2)]
    return lax.ppermute(value, "date", pairs + [(b, a) for a, b in pairs])


def pair_tables(date_pairs, assignment, myself, owners, local_dates):
    anchor = myself * local_dates - 2
    first = date_pairs[:, 0] - anchor
    second = date_pairs[:, 1] - anchor
    known = jnp.array(KNOWN, jnp.int32)
    flipped = (known[:, 2] == 1) == (myself % 2 == 1)
    known_first = jnp.where(flipped, 7 - known[:, 0], known[:, 0])[None, :]
    known_second = jnp.where(flipped, 7 - known[:, 1], known[:, 1])[None, :]
    first, second = first[:, None], second[:, None]
    forward = (first == known_first) & (second == known_second)
    backward = (first == known_second) & (second == known_first)
    is_edge = forward | backward
    count = jnp.sum(is_edge.astype(jnp.int32), axis=0)
    edge = jnp.sum(jnp.where(is_edge, jnp.arange(len(KNOWN))[None, :], 0), axis=1)
    way = jnp.sum(forward.astype(jnp.int32) - backward.astype(jnp.int32), axis=1)
    mine = date_pairs[:, 0] // local_dates == myself
    matches = (assignment[None, :] // owners == jnp.arange(owners)[:, None]) & mine[None, :]
    slot = jnp.sum(jnp.where(matches, edge[None, :], 0), axis=1)
    sign = jnp.sum(jnp.where(matches, way[None, :], 0), axis=1)
    return jnp.concatenate([(myself % 2)[None], slot, sign, count]).astype(jnp.int32)


def row_groups(tiles, cells):
    held = [t * TILE + r for t in tiles for r in range(TILE)]
    groups, owners = [], []
    for m in range(cells):
        local = [n for n, row in enumerate(held) if row // ALOOK == m]
        if local:
            groups.append((local[0], local[-1] + 1))
            owners.append(m)
    return groups, owners


def on_device(images, date_pairs, assignment):
    owners = lax.axis_size("date")
    myself = lax.axis_index("date")
    _, local_dates, rows, columns = images.shape
    cells = rows // ALOOK
    cell_count = cells * (columns // RLOOK)
    tiles = rows // TILE
    pieces = ((0,) + tuple(range(3, tiles)), (1, 2))
    runs = (((0, 0, TILE), (3 * TILE, TILE, rows - 3 * TILE)), ((TILE, 0, 2 * TILE),))
    odd = (myself % 2).astype(jnp.int32)[None]
    even = 1 - odd

    packed = packed_rows(odd, images, runs[0], 40)
    later, packed = lax.optimization_barrier((images, packed))
    across = [swapped_across(packed)]
    beside = swapped_beside(later)
    scalars = pair_tables(date_pairs, assignment, myself, owners, local_dates)

    all_groups = row_groups(range(tiles), cells)[0]
    own_source = (images, (2, local_dates, rows), (0, 0, 0))
    own_places = {
        2 + d: [(0, d, t * TILE) for t in range(tiles)] for d in range(local_dates)
    }
    inner = looked_products(
        even, INNER, OWN_PLACES, [own_source], own_places, all_groups, rows, columns
    )
    later, inner = lax.optimization_barrier((images, inner))
    across.append(swapped_across(packed_rows(odd, later, runs[1], 40)))

    side_places = own_places | {
        d: [(1, local_dates - 2 + d, t * TILE) for t in range(tiles)] for d in range(2)
    }
    beside_looked = looked_products(
        even,
        SIDE,
        NEAR_PLACES,
        [own_source, (beside, (2, local_dates, rows), (0, 0, 0))],
        side_places,
        all_groups,
        rows,
        columns,
    )
    later, beside_looked = lax.optimization_barrier((images, beside_looked))
    layout = [[None, None] for _ in range(cells)]
    across_looked = []
    for n, (piece, arrived) in enumerate(zip(pieces, across)):
        size = len(piece)
        sources = [(arrived, (2, 2, size * TILE), (0, 0, 0))]
        sources += [(later, (2, local_dates, TILE), (0, 0, t)) for t in piece]
        places = {d: [(0, d, t * TILE) for t in range(size)] for d in range(2)}
        places |= {2 + d: [(1 + t, d, 0) for t in range(size)] for d in range(local_dates)}
        groups, where = row_groups(piece, cells)
        for g, m in enumerate(where):
            layout[m][n] = g
        across_looked.append(
            looked_products(odd, SIDE, NEAR_PLACES, sources, places, groups, size * TILE, columns)
        )

    def edge_cells(cut):
        return jnp.concatenate([inner[cut], beside_looked[cut], across_looked[0][cut]], axis=1)

    before = shifted(edge_cells(slice(-1, None)), "strip", 1)
    after = shifted(edge_cells(slice(0, 1)), "strip", -1)
    formed, across_back, beside_back = coherences(
        layout, inner, beside_looked, *across_looked, before, after
    )
    tables = (formed, swapped_across(across_back), swapped_beside(beside_back))
    outgoing, sums = slots_and_sums(scalars, tables, owners, local_dates, cell_count)
    table = lax.all_to_all(outgoing, "date", split_axis=0, concat_axis=0, tiled=True)
    return (as_table(table, cell_count), sums)


def solution(mesh):
    return jax.shard_map(
        on_device,
        mesh=mesh,
        in_specs=(P(None, "date", "strip", None), P(), P()),
        out_specs=(P(None, "date", "strip"), P(None, "date", "strip")),
        check_vma=False,
    )
```

```python
import functools

import jax
import jax.numpy as jnp
from jax import lax
from jax.experimental import pallas as pl
from jax.experimental.pallas import tpu as pltpu
from jax.sharding import PartitionSpec as P

ALOOK = 5
RLOOK = 20
LANES = 128
TILE = 16
COLUMNS = 1280
WIDTHS = (1280, 2560)
FIXED = 32000.0
EPS_POWER = 1e-06
MIB = 2**20

INNER = ((2, 3), (2, 4), (2, 5), (3, 4), (3, 5), (4, 5))
SIDE = ((0, 4), (1, 4), (1, 5), (0, 2), (0, 3), (1, 2))
BACK = 4
RETURNED = tuple((3 - i, 3 - j) for i, j in SIDE[:BACK])
OWN_PLACES = (2, 3, 4, 5)
NEAR_PLACES = (0, 1)
KNOWN = tuple(
    (i, j, across)
    for edges, across in ((INNER, 0), (SIDE, 0), (SIDE, 1), (RETURNED, 1), (RETURNED, 0))
    for i, j in edges
)
FORMED = len(INNER) + 2 * len(SIDE)


def products_kernel(edges, powers, places, groups, width, *refs):
    flip = refs[0][0]
    out_ref, look_ref, acc_ref = refs[-3:]
    total = 2 * len(edges) + len(powers)
    tiles = acc_ref.shape[0] // (total * TILE)
    steps = look_ref.shape[0] // width
    step = pl.program_id(0)
    used = sorted({k for e in edges for k in e} | set(powers))

    @pl.when(step == 0)
    def _():
        column = lax.broadcasted_iota(jnp.int32, look_ref.shape, 0)
        begin = lax.broadcasted_iota(jnp.int32, look_ref.shape, 1) * RLOOK
        inside = (column >= begin) & (column < begin + RLOOK)
        look_ref[...] = inside.astype(jnp.float32).astype(jnp.bfloat16)

    def planes(tile, start):
        pixel = {}
        for k in used:
            source, date, row = places[k][tile]
            ref = refs[1 + source]
            date = date + flip * (ref.shape[1] - 1 - 2 * date)
            pixel[k] = tuple(
                ref[c, date, row : row + TILE, start : start + LANES].astype(jnp.float32)
                for c in (0, 1)
            )
        results = []
        for i, j in edges:
            results.append(pixel[i][0] * pixel[j][0] + pixel[i][1] * pixel[j][1])
        for i, j in edges:
            results.append(pixel[i][1] * pixel[j][0] - pixel[i][0] * pixel[j][1])
        for k in powers:
            results.append(pixel[k][0] * pixel[k][0] + pixel[k][1] * pixel[k][1])
        return jnp.concatenate([r.astype(jnp.bfloat16) for r in results], axis=0)

    look = look_ref[pl.ds(pl.multiple_of(step % steps * width, width), width), :]
    for tile in range(tiles):
        formed = jnp.concatenate([planes(tile, s) for s in range(0, width, LANES)], axis=1)
        part = jnp.dot(formed, look, preferred_element_type=jnp.float32)
        span = slice(tile * total * TILE, (tile + 1) * total * TILE)
        if steps > 1:
            part = part + jnp.where(step % steps > 0, acc_ref[span, :], 0.0)
        acc_ref[span, :] = part

    @pl.when(step % steps == steps - 1)
    def _():
        for m, (first, last) in enumerate(groups):
            for p in range(0, total, 8):
                size = min(8, total - p)

                def plane_rows(row):
                    start = (row // TILE * total + p) * TILE + row % TILE
                    return acc_ref[pl.ds(start, size, stride=TILE), :]

                value = plane_rows(first)
                for row in range(first + 1, last):
                    value += plane_rows(row)
                out_ref[m, p : p + size, :] = value


def looked_products(flip, edges, powers, sources, places, groups, rows, columns, width):
    total = 2 * len(edges) + len(powers)
    steps = LANES * RLOOK // width

    def spec(block, index):
        return pl.BlockSpec(block + (width,), lambda i: index + (i,))

    return pl.pallas_call(
        functools.partial(products_kernel, edges, powers, places, groups, width),
        out_shape=jax.ShapeDtypeStruct((len(groups), total, columns // RLOOK), jnp.float32),
        grid=(columns // width,),
        in_specs=[pl.BlockSpec(memory_space=pltpu.SMEM)] + [spec(*s[1:]) for s in sources],
        out_specs=pl.BlockSpec((len(groups), total, LANES), lambda i: (0, 0, i // steps)),
        scratch_shapes=[
            pltpu.VMEM((LANES * RLOOK, LANES), jnp.bfloat16),
            pltpu.VMEM((total * rows, LANES), jnp.float32),
        ],
        compiler_params=pltpu.CompilerParams(vmem_limit_bytes=48 * MIB),
    )(flip, *[s[0] for s in sources])


def pack_kernel(runs, flip_ref, images_ref, out_ref, semaphores):
    first = 2 * flip_ref[0]
    copies = []
    for c in range(2):
        for row, target, size in runs:
            copies.append(
                pltpu.make_async_copy(
                    images_ref.at[c, pl.ds(first, 2), row : row + size, :],
                    out_ref.at[c, :, target : target + size, :],
                    semaphores.at[len(copies)],
                )
            )
    for copy in copies:
        copy.start()
    for copy in copies:
        copy.wait()


def packed_rows(flip, images, runs, limit):
    columns = images.shape[3]
    rows = sum(size for _, _, size in runs)
    return pl.pallas_call(
        functools.partial(pack_kernel, runs),
        out_shape=jax.ShapeDtypeStruct((2, 2, rows, columns), images.dtype),
        in_specs=[pl.BlockSpec(memory_space=pltpu.SMEM), pl.BlockSpec(memory_space=pl.ANY)],
        out_specs=pl.BlockSpec(memory_space=pltpu.VMEM),
        scratch_shapes=[pltpu.SemaphoreType.DMA((2 * len(runs),))],
        compiler_params=pltpu.CompilerParams(vmem_limit_bytes=limit * MIB),
    )(flip, images)


def coherence_kernel(layout, *refs):
    inner_ref, beside_ref, first_ref, second_ref, before_ref, after_ref = refs[:6]
    formed_ref, across_back_ref, beside_back_ref = refs[6:]
    cells, n_first, width = inner_ref.shape
    n_second = beside_ref.shape[1]
    halves = width // LANES
    block = 2 * cells * halves

    def padded(at, start, size):
        planes = slice(start, start + size)
        return (
            [before_ref[0, planes]] + [at(m) for m in range(cells)] + [after_ref[0, planes]]
        )

    def across_at(m):
        return sum(ref[n] for ref, n in zip((first_ref, second_ref), layout[m]) if n is not None)

    rows = (
        padded(lambda m: inner_ref[m], 0, n_first),
        padded(lambda m: beside_ref[m], n_first, n_second),
        padded(across_at, n_first + n_second, n_second),
    )
    for m in range(cells):
        inner, beside, across = (r[m] + 2.0 * r[m + 1] + r[m + 2] for r in rows)

        def power_of(smooth, edges, n):
            return smooth[2 * len(edges) + n : 2 * len(edges) + n + 1]

        beside_power = {k: power_of(beside, SIDE, n) for n, k in enumerate(NEAR_PLACES)}
        across_power = {k: power_of(across, SIDE, n) for n, k in enumerate(NEAR_PLACES)}
        for n, k in enumerate(OWN_PLACES):
            beside_power[k] = power_of(inner, INNER, n)
            across_power[7 - k] = beside_power[k]
        start = 0
        for values, edges, power in (
            (inner, INNER, beside_power),
            (beside, SIDE, beside_power),
            (across, SIDE, across_power),
        ):
            size = len(edges)
            first = jnp.concatenate([power[i] for i, _ in edges], axis=0)
            second = jnp.concatenate([power[j] for _, j in edges], axis=0)
            scale = lax.rsqrt(first * second + EPS_POWER)
            for part in range(2):
                value = values[part * size : (part + 1) * size] * scale
                for h in range(halves):
                    row = (part * cells + m) * halves + h
                    piece = value[:, h * LANES : (h + 1) * LANES]
                    formed_ref[pl.ds(start * block + row, size, stride=block), :] = piece
            start += size
    size = BACK * block
    for back_ref, first in (
        (beside_back_ref, len(INNER) * block),
        (across_back_ref, (len(INNER) + len(SIDE)) * block),
    ):
        fixed = jnp.round(formed_ref[first : first + size, :] * FIXED)
        back_ref[...] = fixed.astype(jnp.int32).astype(jnp.int16)


def coherences(layout, inner, beside, first, second, before, after):
    cells, _, width = inner.shape
    block = 2 * cells * (width // LANES)
    return pl.pallas_call(
        functools.partial(coherence_kernel, layout),
        out_shape=[
            jax.ShapeDtypeStruct((n * block, LANES), dtype)
            for n, dtype in ((FORMED, jnp.float32), (BACK, jnp.int16), (BACK, jnp.int16))
        ],
        compiler_params=pltpu.CompilerParams(vmem_limit_bytes=32 * MIB),
    )(inner, beside, first, second, before, after)


def slots_kernel(scalar_ref, *refs):
    out_ref, sums_ref, known_ref, rows_ref = refs[-4:]
    owners, block, _ = out_ref.shape
    odd = scalar_ref[0]
    start = 0
    for table in refs[:-4]:
        value = table[...]
        if table.dtype == jnp.int16:
            value = value.astype(jnp.int32).astype(jnp.float32) * (1.0 / FIXED)
        known_ref[start : start + table.shape[0], :] = value
        start += table.shape[0]
    for o in range(owners):
        row = pl.multiple_of(scalar_ref[1 + o] * block, block)
        value = known_ref[pl.ds(row, block), :]
        half = block // 2
        sign = scalar_ref[1 + owners + o].astype(jnp.float32)
        scales = (jnp.abs(sign) * FIXED, sign * FIXED)
        for part in range(2):
            fixed = jnp.round(value[part * half : (part + 1) * half] * scales[part])
            out_ref[o, part * half : (part + 1) * half, :] = fixed.astype(jnp.int32).astype(jnp.int16)
    parts, dates, cell_count = sums_ref.shape
    tiles = cell_count // LANES
    for part in range(parts):
        totals = {k: jnp.zeros((tiles, LANES), jnp.float32) for k in OWN_PLACES}
        for e, (first, second, across) in enumerate(KNOWN):
            row = (e * parts + part) * tiles
            count = scalar_ref[1 + 2 * owners + e].astype(jnp.float32)
            value = known_ref[row : row + tiles, :] * count
            for k in OWN_PLACES:
                place = k if across else 7 - k
                if place == first or (place == second and part == 0):
                    totals[k] = totals[k] + value
                elif place == second:
                    totals[k] = totals[k] - value
        for d, k in enumerate(OWN_PLACES):
            date = d + odd * (dates - 1 - 2 * d)
            first = pl.multiple_of((part * dates + date) * tiles, tiles)
            rows_ref[pl.ds(first, tiles), :] = totals[k]
    for part in range(parts):
        for t in range(tiles):
            sums_ref[part, :, t * LANES : (t + 1) * LANES] = rows_ref[
                pl.ds(part * dates * tiles + t, dates, stride=tiles), :
            ]


def slots_and_sums(scalars, tables, owners, local_dates, cell_count):
    smem = pl.BlockSpec(memory_space=pltpu.SMEM)
    vmem = pl.BlockSpec(memory_space=pltpu.VMEM)
    block = 2 * cell_count // LANES
    return pl.pallas_call(
        slots_kernel,
        out_shape=[
            jax.ShapeDtypeStruct((owners, block, LANES), jnp.int16),
            jax.ShapeDtypeStruct((2, local_dates, cell_count), jnp.float32),
        ],
        in_specs=[smem] + [vmem] * len(tables),
        scratch_shapes=[
            pltpu.VMEM((len(KNOWN) * block, LANES), jnp.float32),
            pltpu.VMEM((local_dates * block, LANES), jnp.float32),
        ],
        compiler_params=pltpu.CompilerParams(vmem_limit_bytes=32 * MIB),
    )(scalars, *tables)


def table_kernel(arrived_ref, out_ref, rows_ref):
    parts, owners, cell_count = out_ref.shape
    tiles = cell_count // LANES
    for o in range(owners):
        rows_ref[o * parts * tiles : (o + 1) * parts * tiles, :] = arrived_ref[o].astype(
            jnp.int32
        ).astype(jnp.float32) * (1.0 / FIXED)
    for part in range(parts):
        for t in range(tiles):
            out_ref[part, :, t * LANES : (t + 1) * LANES] = rows_ref[
                pl.ds(part * tiles + t, owners, stride=parts * tiles), :
            ]


def as_table(arrived, cell_count):
    owners, block, _ = arrived.shape
    return pl.pallas_call(
        table_kernel,
        out_shape=jax.ShapeDtypeStruct((2, owners, cell_count), jnp.float32),
        scratch_shapes=[pltpu.VMEM((owners * block, LANES), jnp.float32)],
        compiler_params=pltpu.CompilerParams(vmem_limit_bytes=32 * MIB),
    )(arrived)


def shifted(value, axis, steps):
    count = lax.axis_size(axis)
    first, last = (max(0, -steps), min(count, count - steps))
    return lax.ppermute(value, axis, [(source, source + steps) for source in range(first, last)])


def swapped_across(value):
    pairs = [(i, i + 1) for i in range(1, lax.axis_size("date") - 1, 2)]
    return lax.ppermute(value, "date", pairs + [(b, a) for a, b in pairs])


def swapped_beside(value):
    pairs = [(i, i + 1) for i in range(0, lax.axis_size("date"), 2)]
    return lax.ppermute(value, "date", pairs + [(b, a) for a, b in pairs])


def pair_tables(date_pairs, assignment, myself, owners, local_dates):
    anchor = myself * local_dates - 2
    first = date_pairs[:, 0] - anchor
    second = date_pairs[:, 1] - anchor
    known = jnp.array(KNOWN, jnp.int32)
    flipped = (known[:, 2] == 1) == (myself % 2 == 1)
    known_first = jnp.where(flipped, 7 - known[:, 0], known[:, 0])[None, :]
    known_second = jnp.where(flipped, 7 - known[:, 1], known[:, 1])[None, :]
    first, second = first[:, None], second[:, None]
    forward = (first == known_first) & (second == known_second)
    backward = (first == known_second) & (second == known_first)
    is_edge = forward | backward
    count = jnp.sum(is_edge.astype(jnp.int32), axis=0)
    edge = jnp.sum(jnp.where(is_edge, jnp.arange(len(KNOWN))[None, :], 0), axis=1)
    way = jnp.sum(forward.astype(jnp.int32) - backward.astype(jnp.int32), axis=1)
    mine = date_pairs[:, 0] // local_dates == myself
    matches = (assignment[None, :] // owners == jnp.arange(owners)[:, None]) & mine[None, :]
    slot = jnp.sum(jnp.where(matches, edge[None, :], 0), axis=1)
    sign = jnp.sum(jnp.where(matches, way[None, :], 0), axis=1)
    return jnp.concatenate([(myself % 2)[None], slot, sign, count]).astype(jnp.int32)


def row_groups(tiles, cells):
    held = [t * TILE + r for t in tiles for r in range(TILE)]
    groups, owners = [], []
    for m in range(cells):
        local = [n for n, row in enumerate(held) if row // ALOOK == m]
        if local:
            groups.append((local[0], local[-1] + 1))
            owners.append(m)
    return groups, owners


def on_device(images, date_pairs, assignment):
    owners = lax.axis_size("date")
    myself = lax.axis_index("date")
    _, local_dates, rows, columns = images.shape
    cells = rows // ALOOK
    cell_count = cells * (columns // RLOOK)
    tiles = rows // TILE
    pieces = ((0,) + tuple(range(3, tiles)), (1, 2))
    runs = (((0, 0, TILE), (3 * TILE, TILE, rows - 3 * TILE)), ((TILE, 0, 2 * TILE),))
    odd = (myself % 2).astype(jnp.int32)[None]
    even = 1 - odd

    packed = packed_rows(odd, images, runs[0], 40)
    later, packed = lax.optimization_barrier((images, packed))
    across = [swapped_across(packed)]
    beside = swapped_beside(later)
    scalars = pair_tables(date_pairs, assignment, myself, owners, local_dates)

    all_groups = row_groups(range(tiles), cells)[0]
    own_source = (images, (2, local_dates, rows), (0, 0, 0))
    own_places = {
        2 + d: [(0, d, t * TILE) for t in range(tiles)] for d in range(local_dates)
    }
    inner = looked_products(
        even, INNER, OWN_PLACES, [own_source], own_places, all_groups, rows, columns, COLUMNS
    )
    later, inner = lax.optimization_barrier((images, inner))
    across.append(swapped_across(packed_rows(odd, later, runs[1], 40)))

    side_places = own_places | {
        d: [(1, local_dates - 2 + d, t * TILE) for t in range(tiles)] for d in range(2)
    }
    beside_looked = looked_products(
        even,
        SIDE,
        NEAR_PLACES,
        [own_source, (beside, (2, local_dates, rows), (0, 0, 0))],
        side_places,
        all_groups,
        rows,
        columns,
        COLUMNS,
    )
    later, beside_looked = lax.optimization_barrier((images, beside_looked))
    layout = [[None, None] for _ in range(cells)]
    across_looked = []
    for n, (piece, arrived) in enumerate(zip(pieces, across)):
        size = len(piece)
        sources = [(arrived, (2, 2, size * TILE), (0, 0, 0))]
        sources += [(later, (2, local_dates, TILE), (0, 0, t)) for t in piece]
        places = {d: [(0, d, t * TILE) for t in range(size)] for d in range(2)}
        places |= {2 + d: [(1 + t, d, 0) for t in range(size)] for d in range(local_dates)}
        groups, where = row_groups(piece, cells)
        for g, m in enumerate(where):
            layout[m][n] = g
        across_looked.append(
            looked_products(
                odd,
                SIDE,
                NEAR_PLACES,
                sources,
                places,
                groups,
                size * TILE,
                columns,
                WIDTHS[n],
            )
        )

    def edge_cells(cut):
        return jnp.concatenate([inner[cut], beside_looked[cut], across_looked[0][cut]], axis=1)

    before = shifted(edge_cells(slice(-1, None)), "strip", 1)
    after = shifted(edge_cells(slice(0, 1)), "strip", -1)
    formed, across_back, beside_back = coherences(
        layout, inner, beside_looked, *across_looked, before, after
    )
    tables = (formed, swapped_across(across_back), swapped_beside(beside_back))
    outgoing, sums = slots_and_sums(scalars, tables, owners, local_dates, cell_count)
    table = lax.all_to_all(outgoing, "date", split_axis=0, concat_axis=0, tiled=True)
    return (as_table(table, cell_count), sums)


def solution(mesh):
    return jax.shard_map(
        on_device,
        mesh=mesh,
        in_specs=(P(None, "date", "strip", None), P(), P()),
        out_specs=(P(None, "date", "strip"), P(None, "date", "strip")),
        check_vma=False,
    )
```

```python
import functools

import jax
import jax.numpy as jnp
from jax import lax
from jax.experimental import pallas as pl
from jax.experimental.pallas import tpu as pltpu
from jax.sharding import PartitionSpec as P

ALOOK = 5
RLOOK = 20
LANES = 128
TILE = 16
COLUMNS = 2560
WIDTHS = (2560, 2560)
FIXED = 32000.0
EPS_POWER = 1e-06
MIB = 2**20

INNER = ((2, 3), (2, 4), (2, 5), (3, 4), (3, 5), (4, 5))
SIDE = ((0, 4), (1, 4), (1, 5), (0, 2), (0, 3), (1, 2))
BACK = 4
RETURNED = tuple((3 - i, 3 - j) for i, j in SIDE[:BACK])
OWN_PLACES = (2, 3, 4, 5)
NEAR_PLACES = (0, 1)
KNOWN = tuple(
    (i, j, across)
    for edges, across in ((INNER, 0), (SIDE, 0), (SIDE, 1), (RETURNED, 1), (RETURNED, 0))
    for i, j in edges
)
FORMED = len(INNER) + 2 * len(SIDE)


def products_kernel(edges, powers, places, groups, width, *refs):
    flip = refs[0][0]
    out_ref, look_ref, acc_ref = refs[-3:]
    total = 2 * len(edges) + len(powers)
    tiles = acc_ref.shape[0] // (total * TILE)
    steps = look_ref.shape[0] // width
    step = pl.program_id(0)
    used = sorted({k for e in edges for k in e} | set(powers))

    @pl.when(step == 0)
    def _():
        column = lax.broadcasted_iota(jnp.int32, look_ref.shape, 0)
        begin = lax.broadcasted_iota(jnp.int32, look_ref.shape, 1) * RLOOK
        inside = (column >= begin) & (column < begin + RLOOK)
        look_ref[...] = inside.astype(jnp.float32).astype(jnp.bfloat16)

    def planes(tile, start):
        pixel = {}
        for k in used:
            source, date, row = places[k][tile]
            ref = refs[1 + source]
            date = date + flip * (ref.shape[1] - 1 - 2 * date)
            pixel[k] = tuple(
                ref[c, date, row : row + TILE, start : start + LANES].astype(jnp.float32)
                for c in (0, 1)
            )
        results = []
        for i, j in edges:
            results.append(pixel[i][0] * pixel[j][0] + pixel[i][1] * pixel[j][1])
        for i, j in edges:
            results.append(pixel[i][1] * pixel[j][0] - pixel[i][0] * pixel[j][1])
        for k in powers:
            results.append(pixel[k][0] * pixel[k][0] + pixel[k][1] * pixel[k][1])
        return jnp.concatenate([r.astype(jnp.bfloat16) for r in results], axis=0)

    look = look_ref[pl.ds(pl.multiple_of(step % steps * width, width), width), :]
    for tile in range(tiles):
        formed = jnp.concatenate([planes(tile, s) for s in range(0, width, LANES)], axis=1)
        part = jnp.dot(formed, look, preferred_element_type=jnp.float32)
        span = slice(tile * total * TILE, (tile + 1) * total * TILE)
        if steps > 1:
            part = part + jnp.where(step % steps > 0, acc_ref[span, :], 0.0)
        acc_ref[span, :] = part

    @pl.when(step % steps == steps - 1)
    def _():
        for m, (first, last) in enumerate(groups):
            for p in range(0, total, 8):
                size = min(8, total - p)

                def plane_rows(row):
                    start = (row // TILE * total + p) * TILE + row % TILE
                    return acc_ref[pl.ds(start, size, stride=TILE), :]

                value = plane_rows(first)
                for row in range(first + 1, last):
                    value += plane_rows(row)
                out_ref[m, p : p + size, :] = value


def looked_products(flip, edges, powers, sources, places, groups, rows, columns, width):
    total = 2 * len(edges) + len(powers)
    steps = LANES * RLOOK // width

    def spec(block, index):
        return pl.BlockSpec(block + (width,), lambda i: index + (i,))

    return pl.pallas_call(
        functools.partial(products_kernel, edges, powers, places, groups, width),
        out_shape=jax.ShapeDtypeStruct((len(groups), total, columns // RLOOK), jnp.float32),
        grid=(columns // width,),
        in_specs=[pl.BlockSpec(memory_space=pltpu.SMEM)] + [spec(*s[1:]) for s in sources],
        out_specs=pl.BlockSpec((len(groups), total, LANES), lambda i: (0, 0, i // steps)),
        scratch_shapes=[
            pltpu.VMEM((LANES * RLOOK, LANES), jnp.bfloat16),
            pltpu.VMEM((total * rows, LANES), jnp.float32),
        ],
        compiler_params=pltpu.CompilerParams(vmem_limit_bytes=48 * MIB),
    )(flip, *[s[0] for s in sources])


def pack_kernel(runs, flip_ref, images_ref, out_ref, semaphores):
    first = 2 * flip_ref[0]
    copies = []
    for c in range(2):
        for row, target, size in runs:
            copies.append(
                pltpu.make_async_copy(
                    images_ref.at[c, pl.ds(first, 2), row : row + size, :],
                    out_ref.at[c, :, target : target + size, :],
                    semaphores.at[len(copies)],
                )
            )
    for copy in copies:
        copy.start()
    for copy in copies:
        copy.wait()


def packed_rows(flip, images, runs, limit):
    columns = images.shape[3]
    rows = sum(size for _, _, size in runs)
    return pl.pallas_call(
        functools.partial(pack_kernel, runs),
        out_shape=jax.ShapeDtypeStruct((2, 2, rows, columns), images.dtype),
        in_specs=[pl.BlockSpec(memory_space=pltpu.SMEM), pl.BlockSpec(memory_space=pl.ANY)],
        out_specs=pl.BlockSpec(memory_space=pltpu.VMEM),
        scratch_shapes=[pltpu.SemaphoreType.DMA((2 * len(runs),))],
        compiler_params=pltpu.CompilerParams(vmem_limit_bytes=limit * MIB),
    )(flip, images)


def coherence_kernel(layout, *refs):
    inner_ref, beside_ref, first_ref, second_ref, before_ref, after_ref = refs[:6]
    formed_ref, across_back_ref, beside_back_ref = refs[6:]
    cells, n_first, width = inner_ref.shape
    n_second = beside_ref.shape[1]
    halves = width // LANES
    block = 2 * cells * halves

    def padded(at, start, size):
        planes = slice(start, start + size)
        return (
            [before_ref[0, planes]] + [at(m) for m in range(cells)] + [after_ref[0, planes]]
        )

    def across_at(m):
        return sum(ref[n] for ref, n in zip((first_ref, second_ref), layout[m]) if n is not None)

    rows = (
        padded(lambda m: inner_ref[m], 0, n_first),
        padded(lambda m: beside_ref[m], n_first, n_second),
        padded(across_at, n_first + n_second, n_second),
    )
    for m in range(cells):
        inner, beside, across = (r[m] + 2.0 * r[m + 1] + r[m + 2] for r in rows)

        def power_of(smooth, edges, n):
            return smooth[2 * len(edges) + n : 2 * len(edges) + n + 1]

        beside_power = {k: power_of(beside, SIDE, n) for n, k in enumerate(NEAR_PLACES)}
        across_power = {k: power_of(across, SIDE, n) for n, k in enumerate(NEAR_PLACES)}
        for n, k in enumerate(OWN_PLACES):
            beside_power[k] = power_of(inner, INNER, n)
            across_power[7 - k] = beside_power[k]
        start = 0
        for values, edges, power in (
            (inner, INNER, beside_power),
            (beside, SIDE, beside_power),
            (across, SIDE, across_power),
        ):
            size = len(edges)
            first = jnp.concatenate([power[i] for i, _ in edges], axis=0)
            second = jnp.concatenate([power[j] for _, j in edges], axis=0)
            scale = lax.rsqrt(first * second + EPS_POWER)
            for part in range(2):
                value = values[part * size : (part + 1) * size] * scale
                for h in range(halves):
                    row = (part * cells + m) * halves + h
                    piece = value[:, h * LANES : (h + 1) * LANES]
                    formed_ref[pl.ds(start * block + row, size, stride=block), :] = piece
            start += size
    size = BACK * block
    for back_ref, first in (
        (beside_back_ref, len(INNER) * block),
        (across_back_ref, (len(INNER) + len(SIDE)) * block),
    ):
        fixed = jnp.round(formed_ref[first : first + size, :] * FIXED)
        back_ref[...] = fixed.astype(jnp.int32).astype(jnp.int16)


def coherences(layout, inner, beside, first, second, before, after):
    cells, _, width = inner.shape
    block = 2 * cells * (width // LANES)
    return pl.pallas_call(
        functools.partial(coherence_kernel, layout),
        out_shape=[
            jax.ShapeDtypeStruct((n * block, LANES), dtype)
            for n, dtype in ((FORMED, jnp.float32), (BACK, jnp.int16), (BACK, jnp.int16))
        ],
        compiler_params=pltpu.CompilerParams(vmem_limit_bytes=32 * MIB),
    )(inner, beside, first, second, before, after)


def slots_kernel(scalar_ref, *refs):
    out_ref, sums_ref, known_ref, rows_ref = refs[-4:]
    owners, block, _ = out_ref.shape
    odd = scalar_ref[0]
    start = 0
    for table in refs[:-4]:
        value = table[...]
        if table.dtype == jnp.int16:
            value = value.astype(jnp.int32).astype(jnp.float32) * (1.0 / FIXED)
        known_ref[start : start + table.shape[0], :] = value
        start += table.shape[0]
    for o in range(owners):
        row = pl.multiple_of(scalar_ref[1 + o] * block, block)
        value = known_ref[pl.ds(row, block), :]
        half = block // 2
        sign = scalar_ref[1 + owners + o].astype(jnp.float32)
        scales = (jnp.abs(sign) * FIXED, sign * FIXED)
        for part in range(2):
            fixed = jnp.round(value[part * half : (part + 1) * half] * scales[part])
            out_ref[o, part * half : (part + 1) * half, :] = fixed.astype(jnp.int32).astype(jnp.int16)
    parts, dates, cell_count = sums_ref.shape
    tiles = cell_count // LANES
    for part in range(parts):
        totals = {k: jnp.zeros((tiles, LANES), jnp.float32) for k in OWN_PLACES}
        for e, (first, second, across) in enumerate(KNOWN):
            row = (e * parts + part) * tiles
            count = scalar_ref[1 + 2 * owners + e].astype(jnp.float32)
            value = known_ref[row : row + tiles, :] * count
            for k in OWN_PLACES:
                place = k if across else 7 - k
                if place == first or (place == second and part == 0):
                    totals[k] = totals[k] + value
                elif place == second:
                    totals[k] = totals[k] - value
        for d, k in enumerate(OWN_PLACES):
            date = d + odd * (dates - 1 - 2 * d)
            first = pl.multiple_of((part * dates + date) * tiles, tiles)
            rows_ref[pl.ds(first, tiles), :] = totals[k]
    for part in range(parts):
        for t in range(tiles):
            sums_ref[part, :, t * LANES : (t + 1) * LANES] = rows_ref[
                pl.ds(part * dates * tiles + t, dates, stride=tiles), :
            ]


def slots_and_sums(scalars, tables, owners, local_dates, cell_count):
    smem = pl.BlockSpec(memory_space=pltpu.SMEM)
    vmem = pl.BlockSpec(memory_space=pltpu.VMEM)
    block = 2 * cell_count // LANES
    return pl.pallas_call(
        slots_kernel,
        out_shape=[
            jax.ShapeDtypeStruct((owners, block, LANES), jnp.int16),
            jax.ShapeDtypeStruct((2, local_dates, cell_count), jnp.float32),
        ],
        in_specs=[smem] + [vmem] * len(tables),
        scratch_shapes=[
            pltpu.VMEM((len(KNOWN) * block, LANES), jnp.float32),
            pltpu.VMEM((local_dates * block, LANES), jnp.float32),
        ],
        compiler_params=pltpu.CompilerParams(vmem_limit_bytes=32 * MIB),
    )(scalars, *tables)


def table_kernel(arrived_ref, out_ref, rows_ref):
    parts, owners, cell_count = out_ref.shape
    tiles = cell_count // LANES
    for o in range(owners):
        rows_ref[o * parts * tiles : (o + 1) * parts * tiles, :] = arrived_ref[o].astype(
            jnp.int32
        ).astype(jnp.float32) * (1.0 / FIXED)
    for part in range(parts):
        for t in range(tiles):
            out_ref[part, :, t * LANES : (t + 1) * LANES] = rows_ref[
                pl.ds(part * tiles + t, owners, stride=parts * tiles), :
            ]


def as_table(arrived, cell_count):
    owners, block, _ = arrived.shape
    return pl.pallas_call(
        table_kernel,
        out_shape=jax.ShapeDtypeStruct((2, owners, cell_count), jnp.float32),
        scratch_shapes=[pltpu.VMEM((owners * block, LANES), jnp.float32)],
        compiler_params=pltpu.CompilerParams(vmem_limit_bytes=32 * MIB),
    )(arrived)


def shifted(value, axis, steps):
    count = lax.axis_size(axis)
    first, last = (max(0, -steps), min(count, count - steps))
    return lax.ppermute(value, axis, [(source, source + steps) for source in range(first, last)])


def swapped_across(value):
    pairs = [(i, i + 1) for i in range(1, lax.axis_size("date") - 1, 2)]
    return lax.ppermute(value, "date", pairs + [(b, a) for a, b in pairs])


def swapped_beside(value):
    pairs = [(i, i + 1) for i in range(0, lax.axis_size("date"), 2)]
    return lax.ppermute(value, "date", pairs + [(b, a) for a, b in pairs])


def pair_tables(date_pairs, assignment, myself, owners, local_dates):
    anchor = myself * local_dates - 2
    first = date_pairs[:, 0] - anchor
    second = date_pairs[:, 1] - anchor
    known = jnp.array(KNOWN, jnp.int32)
    flipped = (known[:, 2] == 1) == (myself % 2 == 1)
    known_first = jnp.where(flipped, 7 - known[:, 0], known[:, 0])[None, :]
    known_second = jnp.where(flipped, 7 - known[:, 1], known[:, 1])[None, :]
    first, second = first[:, None], second[:, None]
    forward = (first == known_first) & (second == known_second)
    backward = (first == known_second) & (second == known_first)
    is_edge = forward | backward
    count = jnp.sum(is_edge.astype(jnp.int32), axis=0)
    edge = jnp.sum(jnp.where(is_edge, jnp.arange(len(KNOWN))[None, :], 0), axis=1)
    way = jnp.sum(forward.astype(jnp.int32) - backward.astype(jnp.int32), axis=1)
    mine = date_pairs[:, 0] // local_dates == myself
    matches = (assignment[None, :] // owners == jnp.arange(owners)[:, None]) & mine[None, :]
    slot = jnp.sum(jnp.where(matches, edge[None, :], 0), axis=1)
    sign = jnp.sum(jnp.where(matches, way[None, :], 0), axis=1)
    return jnp.concatenate([(myself % 2)[None], slot, sign, count]).astype(jnp.int32)


def row_groups(tiles, cells):
    held = [t * TILE + r for t in tiles for r in range(TILE)]
    groups, owners = [], []
    for m in range(cells):
        local = [n for n, row in enumerate(held) if row // ALOOK == m]
        if local:
            groups.append((local[0], local[-1] + 1))
            owners.append(m)
    return groups, owners


def on_device(images, date_pairs, assignment):
    owners = lax.axis_size("date")
    myself = lax.axis_index("date")
    _, local_dates, rows, columns = images.shape
    cells = rows // ALOOK
    cell_count = cells * (columns // RLOOK)
    tiles = rows // TILE
    pieces = ((0,) + tuple(range(3, tiles)), (1, 2))
    runs = (((0, 0, TILE), (3 * TILE, TILE, rows - 3 * TILE)), ((TILE, 0, 2 * TILE),))
    odd = (myself % 2).astype(jnp.int32)[None]
    even = 1 - odd

    packed = packed_rows(odd, images, runs[0], 40)
    later, packed = lax.optimization_barrier((images, packed))
    across = [swapped_across(packed)]
    beside = swapped_beside(later)
    scalars = pair_tables(date_pairs, assignment, myself, owners, local_dates)

    all_groups = row_groups(range(tiles), cells)[0]
    own_source = (images, (2, local_dates, rows), (0, 0, 0))
    own_places = {
        2 + d: [(0, d, t * TILE) for t in range(tiles)] for d in range(local_dates)
    }
    inner = looked_products(
        even, INNER, OWN_PLACES, [own_source], own_places, all_groups, rows, columns, COLUMNS
    )
    later, inner = lax.optimization_barrier((images, inner))
    across.append(swapped_across(packed_rows(odd, later, runs[1], 40)))

    side_places = own_places | {
        d: [(1, local_dates - 2 + d, t * TILE) for t in range(tiles)] for d in range(2)
    }
    beside_looked = looked_products(
        even,
        SIDE,
        NEAR_PLACES,
        [own_source, (beside, (2, local_dates, rows), (0, 0, 0))],
        side_places,
        all_groups,
        rows,
        columns,
        COLUMNS,
    )
    later, beside_looked = lax.optimization_barrier((images, beside_looked))
    layout = [[None, None] for _ in range(cells)]
    across_looked = []
    for n, (piece, arrived) in enumerate(zip(pieces, across)):
        size = len(piece)
        sources = [(arrived, (2, 2, size * TILE), (0, 0, 0))]
        sources += [(later, (2, local_dates, TILE), (0, 0, t)) for t in piece]
        places = {d: [(0, d, t * TILE) for t in range(size)] for d in range(2)}
        places |= {2 + d: [(1 + t, d, 0) for t in range(size)] for d in range(local_dates)}
        groups, where = row_groups(piece, cells)
        for g, m in enumerate(where):
            layout[m][n] = g
        across_looked.append(
            looked_products(
                odd,
                SIDE,
                NEAR_PLACES,
                sources,
                places,
                groups,
                size * TILE,
                columns,
                WIDTHS[n],
            )
        )

    def edge_cells(cut):
        return jnp.concatenate([inner[cut], beside_looked[cut], across_looked[0][cut]], axis=1)

    before = shifted(edge_cells(slice(-1, None)), "strip", 1)
    after = shifted(edge_cells(slice(0, 1)), "strip", -1)
    formed, across_back, beside_back = coherences(
        layout, inner, beside_looked, *across_looked, before, after
    )
    tables = (formed, swapped_across(across_back), swapped_beside(beside_back))
    outgoing, sums = slots_and_sums(scalars, tables, owners, local_dates, cell_count)
    table = lax.all_to_all(outgoing, "date", split_axis=0, concat_axis=0, tiled=True)
    return (as_table(table, cell_count), sums)


def solution(mesh):
    return jax.shard_map(
        on_device,
        mesh=mesh,
        in_specs=(P(None, "date", "strip", None), P(), P()),
        out_specs=(P(None, "date", "strip"), P(None, "date", "strip")),
        check_vma=False,
    )
```

```python
import functools

import jax
import jax.numpy as jnp
from jax import lax
from jax.experimental import pallas as pl
from jax.experimental.pallas import tpu as pltpu
from jax.sharding import PartitionSpec as P

ALOOK = 5
RLOOK = 20
LANES = 128
TILE = 16
COLUMNS = 1280
WIDTHS = (2560, 2560)
FIXED = 32000.0
EPS_POWER = 1e-06
MIB = 2**20

INNER = ((2, 3), (2, 4), (2, 5), (3, 4), (3, 5), (4, 5))
SIDE = ((0, 4), (1, 4), (1, 5), (0, 2), (0, 3), (1, 2))
BACK = 4
RETURNED = tuple((3 - i, 3 - j) for i, j in SIDE[:BACK])
OWN_PLACES = (2, 3, 4, 5)
NEAR_PLACES = (0, 1)
KNOWN = tuple(
    (i, j, across)
    for edges, across in ((INNER, 0), (SIDE, 0), (SIDE, 1), (RETURNED, 1), (RETURNED, 0))
    for i, j in edges
)
FORMED = len(INNER) + 2 * len(SIDE)


def products_kernel(edges, powers, places, groups, width, *refs):
    flip = refs[0][0]
    out_ref, look_ref, acc_ref = refs[-3:]
    total = 2 * len(edges) + len(powers)
    tiles = acc_ref.shape[0] // (total * TILE)
    steps = look_ref.shape[0] // width
    step = pl.program_id(0)
    used = sorted({k for e in edges for k in e} | set(powers))

    @pl.when(step == 0)
    def _():
        column = lax.broadcasted_iota(jnp.int32, look_ref.shape, 0)
        begin = lax.broadcasted_iota(jnp.int32, look_ref.shape, 1) * RLOOK
        inside = (column >= begin) & (column < begin + RLOOK)
        look_ref[...] = inside.astype(jnp.float32).astype(jnp.bfloat16)

    def planes(tile, start):
        pixel = {}
        for k in used:
            source, date, row = places[k][tile]
            ref = refs[1 + source]
            date = date + flip * (ref.shape[1] - 1 - 2 * date)
            pixel[k] = tuple(
                ref[c, date, row : row + TILE, start : start + LANES].astype(jnp.float32)
                for c in (0, 1)
            )
        results = []
        for i, j in edges:
            results.append(pixel[i][0] * pixel[j][0] + pixel[i][1] * pixel[j][1])
        for i, j in edges:
            results.append(pixel[i][1] * pixel[j][0] - pixel[i][0] * pixel[j][1])
        for k in powers:
            results.append(pixel[k][0] * pixel[k][0] + pixel[k][1] * pixel[k][1])
        return jnp.concatenate([r.astype(jnp.bfloat16) for r in results], axis=0)

    look = look_ref[pl.ds(pl.multiple_of(step % steps * width, width), width), :]
    for tile in range(tiles):
        formed = jnp.concatenate([planes(tile, s) for s in range(0, width, LANES)], axis=1)
        part = jnp.dot(formed, look, preferred_element_type=jnp.float32)
        span = slice(tile * total * TILE, (tile + 1) * total * TILE)
        if steps > 1:
            part = part + jnp.where(step % steps > 0, acc_ref[span, :], 0.0)
        acc_ref[span, :] = part

    @pl.when(step % steps == steps - 1)
    def _():
        for m, (first, last) in enumerate(groups):
            for p in range(0, total, 8):
                size = min(8, total - p)

                def plane_rows(row):
                    start = (row // TILE * total + p) * TILE + row % TILE
                    return acc_ref[pl.ds(start, size, stride=TILE), :]

                value = plane_rows(first)
                for row in range(first + 1, last):
                    value += plane_rows(row)
                out_ref[m, p : p + size, :] = value


def looked_products(flip, edges, powers, sources, places, groups, rows, columns, width):
    total = 2 * len(edges) + len(powers)
    steps = LANES * RLOOK // width

    def spec(block, index):
        return pl.BlockSpec(block + (width,), lambda i: index + (i,))

    return pl.pallas_call(
        functools.partial(products_kernel, edges, powers, places, groups, width),
        out_shape=jax.ShapeDtypeStruct((len(groups), total, columns // RLOOK), jnp.float32),
        grid=(columns // width,),
        in_specs=[pl.BlockSpec(memory_space=pltpu.SMEM)] + [spec(*s[1:]) for s in sources],
        out_specs=pl.BlockSpec((len(groups), total, LANES), lambda i: (0, 0, i // steps)),
        scratch_shapes=[
            pltpu.VMEM((LANES * RLOOK, LANES), jnp.bfloat16),
            pltpu.VMEM((total * rows, LANES), jnp.float32),
        ],
        compiler_params=pltpu.CompilerParams(vmem_limit_bytes=48 * MIB),
    )(flip, *[s[0] for s in sources])


def pack_kernel(runs, flip_ref, images_ref, out_ref, semaphores):
    first = 2 * flip_ref[0]
    copies = []
    for c in range(2):
        for row, target, size in runs:
            copies.append(
                pltpu.make_async_copy(
                    images_ref.at[c, pl.ds(first, 2), row : row + size, :],
                    out_ref.at[c, :, target : target + size, :],
                    semaphores.at[len(copies)],
                )
            )
    for copy in copies:
        copy.start()
    for copy in copies:
        copy.wait()


def packed_rows(flip, images, runs, limit):
    columns = images.shape[3]
    rows = sum(size for _, _, size in runs)
    return pl.pallas_call(
        functools.partial(pack_kernel, runs),
        out_shape=jax.ShapeDtypeStruct((2, 2, rows, columns), images.dtype),
        in_specs=[pl.BlockSpec(memory_space=pltpu.SMEM), pl.BlockSpec(memory_space=pl.ANY)],
        out_specs=pl.BlockSpec(memory_space=pltpu.VMEM),
        scratch_shapes=[pltpu.SemaphoreType.DMA((2 * len(runs),))],
        compiler_params=pltpu.CompilerParams(vmem_limit_bytes=limit * MIB),
    )(flip, images)


def coherence_kernel(layout, *refs):
    inner_ref, beside_ref, first_ref, second_ref, before_ref, after_ref = refs[:6]
    formed_ref, across_back_ref, beside_back_ref = refs[6:]
    cells, n_first, width = inner_ref.shape
    n_second = beside_ref.shape[1]
    halves = width // LANES
    block = 2 * cells * halves

    def padded(at, start, size):
        planes = slice(start, start + size)
        return (
            [before_ref[0, planes]] + [at(m) for m in range(cells)] + [after_ref[0, planes]]
        )

    def across_at(m):
        return sum(ref[n] for ref, n in zip((first_ref, second_ref), layout[m]) if n is not None)

    rows = (
        padded(lambda m: inner_ref[m], 0, n_first),
        padded(lambda m: beside_ref[m], n_first, n_second),
        padded(across_at, n_first + n_second, n_second),
    )
    for m in range(cells):
        inner, beside, across = (r[m] + 2.0 * r[m + 1] + r[m + 2] for r in rows)

        def power_of(smooth, edges, n):
            return smooth[2 * len(edges) + n : 2 * len(edges) + n + 1]

        beside_power = {k: power_of(beside, SIDE, n) for n, k in enumerate(NEAR_PLACES)}
        across_power = {k: power_of(across, SIDE, n) for n, k in enumerate(NEAR_PLACES)}
        for n, k in enumerate(OWN_PLACES):
            beside_power[k] = power_of(inner, INNER, n)
            across_power[7 - k] = beside_power[k]
        start = 0
        for values, edges, power in (
            (inner, INNER, beside_power),
            (beside, SIDE, beside_power),
            (across, SIDE, across_power),
        ):
            size = len(edges)
            first = jnp.concatenate([power[i] for i, _ in edges], axis=0)
            second = jnp.concatenate([power[j] for _, j in edges], axis=0)
            scale = lax.rsqrt(first * second + EPS_POWER)
            for part in range(2):
                value = values[part * size : (part + 1) * size] * scale
                for h in range(halves):
                    row = (part * cells + m) * halves + h
                    piece = value[:, h * LANES : (h + 1) * LANES]
                    formed_ref[pl.ds(start * block + row, size, stride=block), :] = piece
            start += size
    size = BACK * block
    for back_ref, first in (
        (beside_back_ref, len(INNER) * block),
        (across_back_ref, (len(INNER) + len(SIDE)) * block),
    ):
        fixed = jnp.round(formed_ref[first : first + size, :] * FIXED)
        back_ref[...] = fixed.astype(jnp.int32).astype(jnp.int16)


def coherences(layout, inner, beside, first, second, before, after):
    cells, _, width = inner.shape
    block = 2 * cells * (width // LANES)
    return pl.pallas_call(
        functools.partial(coherence_kernel, layout),
        out_shape=[
            jax.ShapeDtypeStruct((n * block, LANES), dtype)
            for n, dtype in ((FORMED, jnp.float32), (BACK, jnp.int16), (BACK, jnp.int16))
        ],
        compiler_params=pltpu.CompilerParams(vmem_limit_bytes=32 * MIB),
    )(inner, beside, first, second, before, after)


def slots_kernel(scalar_ref, *refs):
    out_ref, sums_ref, known_ref, rows_ref = refs[-4:]
    owners, block, _ = out_ref.shape
    odd = scalar_ref[0]
    start = 0
    for table in refs[:-4]:
        value = table[...]
        if table.dtype == jnp.int16:
            value = value.astype(jnp.int32).astype(jnp.float32) * (1.0 / FIXED)
        known_ref[start : start + table.shape[0], :] = value
        start += table.shape[0]
    for o in range(owners):
        row = pl.multiple_of(scalar_ref[1 + o] * block, block)
        value = known_ref[pl.ds(row, block), :]
        half = block // 2
        sign = scalar_ref[1 + owners + o].astype(jnp.float32)
        scales = (jnp.abs(sign) * FIXED, sign * FIXED)
        for part in range(2):
            fixed = jnp.round(value[part * half : (part + 1) * half] * scales[part])
            out_ref[o, part * half : (part + 1) * half, :] = fixed.astype(jnp.int32).astype(jnp.int16)
    parts, dates, cell_count = sums_ref.shape
    tiles = cell_count // LANES
    for part in range(parts):
        totals = {k: jnp.zeros((tiles, LANES), jnp.float32) for k in OWN_PLACES}
        for e, (first, second, across) in enumerate(KNOWN):
            row = (e * parts + part) * tiles
            count = scalar_ref[1 + 2 * owners + e].astype(jnp.float32)
            value = known_ref[row : row + tiles, :] * count
            for k in OWN_PLACES:
                place = k if across else 7 - k
                if place == first or (place == second and part == 0):
                    totals[k] = totals[k] + value
                elif place == second:
                    totals[k] = totals[k] - value
        for d, k in enumerate(OWN_PLACES):
            date = d + odd * (dates - 1 - 2 * d)
            first = pl.multiple_of((part * dates + date) * tiles, tiles)
            rows_ref[pl.ds(first, tiles), :] = totals[k]
    for part in range(parts):
        for t in range(tiles):
            sums_ref[part, :, t * LANES : (t + 1) * LANES] = rows_ref[
                pl.ds(part * dates * tiles + t, dates, stride=tiles), :
            ]


def slots_and_sums(scalars, tables, owners, local_dates, cell_count):
    smem = pl.BlockSpec(memory_space=pltpu.SMEM)
    vmem = pl.BlockSpec(memory_space=pltpu.VMEM)
    block = 2 * cell_count // LANES
    return pl.pallas_call(
        slots_kernel,
        out_shape=[
            jax.ShapeDtypeStruct((owners, block, LANES), jnp.int16),
            jax.ShapeDtypeStruct((2, local_dates, cell_count), jnp.float32),
        ],
        in_specs=[smem] + [vmem] * len(tables),
        scratch_shapes=[
            pltpu.VMEM((len(KNOWN) * block, LANES), jnp.float32),
            pltpu.VMEM((local_dates * block, LANES), jnp.float32),
        ],
        compiler_params=pltpu.CompilerParams(vmem_limit_bytes=32 * MIB),
    )(scalars, *tables)


def table_kernel(arrived_ref, out_ref, rows_ref):
    parts, owners, cell_count = out_ref.shape
    tiles = cell_count // LANES
    for o in range(owners):
        rows_ref[o * parts * tiles : (o + 1) * parts * tiles, :] = arrived_ref[o].astype(
            jnp.int32
        ).astype(jnp.float32) * (1.0 / FIXED)
    for part in range(parts):
        for t in range(tiles):
            out_ref[part, :, t * LANES : (t + 1) * LANES] = rows_ref[
                pl.ds(part * tiles + t, owners, stride=parts * tiles), :
            ]


def as_table(arrived, cell_count):
    owners, block, _ = arrived.shape
    return pl.pallas_call(
        table_kernel,
        out_shape=jax.ShapeDtypeStruct((2, owners, cell_count), jnp.float32),
        scratch_shapes=[pltpu.VMEM((owners * block, LANES), jnp.float32)],
        compiler_params=pltpu.CompilerParams(vmem_limit_bytes=32 * MIB),
    )(arrived)


def shifted(value, axis, steps):
    count = lax.axis_size(axis)
    first, last = (max(0, -steps), min(count, count - steps))
    return lax.ppermute(value, axis, [(source, source + steps) for source in range(first, last)])


def swapped_across(value):
    pairs = [(i, i + 1) for i in range(1, lax.axis_size("date") - 1, 2)]
    return lax.ppermute(value, "date", pairs + [(b, a) for a, b in pairs])


def swapped_beside(value):
    pairs = [(i, i + 1) for i in range(0, lax.axis_size("date"), 2)]
    return lax.ppermute(value, "date", pairs + [(b, a) for a, b in pairs])


def pair_tables(date_pairs, assignment, myself, owners, local_dates):
    anchor = myself * local_dates - 2
    first = date_pairs[:, 0] - anchor
    second = date_pairs[:, 1] - anchor
    known = jnp.array(KNOWN, jnp.int32)
    flipped = (known[:, 2] == 1) == (myself % 2 == 1)
    known_first = jnp.where(flipped, 7 - known[:, 0], known[:, 0])[None, :]
    known_second = jnp.where(flipped, 7 - known[:, 1], known[:, 1])[None, :]
    first, second = first[:, None], second[:, None]
    forward = (first == known_first) & (second == known_second)
    backward = (first == known_second) & (second == known_first)
    is_edge = forward | backward
    count = jnp.sum(is_edge.astype(jnp.int32), axis=0)
    edge = jnp.sum(jnp.where(is_edge, jnp.arange(len(KNOWN))[None, :], 0), axis=1)
    way = jnp.sum(forward.astype(jnp.int32) - backward.astype(jnp.int32), axis=1)
    mine = date_pairs[:, 0] // local_dates == myself
    matches = (assignment[None, :] // owners == jnp.arange(owners)[:, None]) & mine[None, :]
    slot = jnp.sum(jnp.where(matches, edge[None, :], 0), axis=1)
    sign = jnp.sum(jnp.where(matches, way[None, :], 0), axis=1)
    return jnp.concatenate([(myself % 2)[None], slot, sign, count]).astype(jnp.int32)


def row_groups(tiles, cells):
    held = [t * TILE + r for t in tiles for r in range(TILE)]
    groups, owners = [], []
    for m in range(cells):
        local = [n for n, row in enumerate(held) if row // ALOOK == m]
        if local:
            groups.append((local[0], local[-1] + 1))
            owners.append(m)
    return groups, owners


def on_device(images, date_pairs, assignment):
    owners = lax.axis_size("date")
    myself = lax.axis_index("date")
    _, local_dates, rows, columns = images.shape
    cells = rows // ALOOK
    cell_count = cells * (columns // RLOOK)
    tiles = rows // TILE
    pieces = ((0,) + tuple(range(3, tiles)), (1, 2))
    runs = (((0, 0, TILE), (3 * TILE, TILE, rows - 3 * TILE)), ((TILE, 0, 2 * TILE),))
    odd = (myself % 2).astype(jnp.int32)[None]
    even = 1 - odd

    packed = packed_rows(odd, images, runs[0], 40)
    later, packed = lax.optimization_barrier((images, packed))
    across = [swapped_across(packed)]
    beside = swapped_beside(later)
    scalars = pair_tables(date_pairs, assignment, myself, owners, local_dates)

    all_groups = row_groups(range(tiles), cells)[0]
    own_source = (images, (2, local_dates, rows), (0, 0, 0))
    own_places = {
        2 + d: [(0, d, t * TILE) for t in range(tiles)] for d in range(local_dates)
    }
    inner = looked_products(
        even, INNER, OWN_PLACES, [own_source], own_places, all_groups, rows, columns, COLUMNS
    )
    later, inner = lax.optimization_barrier((images, inner))
    across.append(swapped_across(packed_rows(odd, later, runs[1], 40)))

    side_places = own_places | {
        d: [(1, local_dates - 2 + d, t * TILE) for t in range(tiles)] for d in range(2)
    }
    beside_looked = looked_products(
        even,
        SIDE,
        NEAR_PLACES,
        [own_source, (beside, (2, local_dates, rows), (0, 0, 0))],
        side_places,
        all_groups,
        rows,
        columns,
        COLUMNS,
    )
    later, beside_looked = lax.optimization_barrier((images, beside_looked))
    layout = [[None, None] for _ in range(cells)]
    across_looked = []
    for n, (piece, arrived) in enumerate(zip(pieces, across)):
        size = len(piece)
        sources = [(arrived, (2, 2, size * TILE), (0, 0, 0))]
        sources += [(later, (2, local_dates, TILE), (0, 0, t)) for t in piece]
        places = {d: [(0, d, t * TILE) for t in range(size)] for d in range(2)}
        places |= {2 + d: [(1 + t, d, 0) for t in range(size)] for d in range(local_dates)}
        groups, where = row_groups(piece, cells)
        for g, m in enumerate(where):
            layout[m][n] = g
        across_looked.append(
            looked_products(
                odd,
                SIDE,
                NEAR_PLACES,
                sources,
                places,
                groups,
                size * TILE,
                columns,
                WIDTHS[n],
            )
        )

    def edge_cells(cut):
        return jnp.concatenate([inner[cut], beside_looked[cut], across_looked[0][cut]], axis=1)

    before = shifted(edge_cells(slice(-1, None)), "strip", 1)
    after = shifted(edge_cells(slice(0, 1)), "strip", -1)
    formed, across_back, beside_back = coherences(
        layout, inner, beside_looked, *across_looked, before, after
    )
    tables = (formed, swapped_across(across_back), swapped_beside(beside_back))
    outgoing, sums = slots_and_sums(scalars, tables, owners, local_dates, cell_count)
    table = lax.all_to_all(outgoing, "date", split_axis=0, concat_axis=0, tiled=True)
    return (as_table(table, cell_count), sums)


def solution(mesh):
    return jax.shard_map(
        on_device,
        mesh=mesh,
        in_specs=(P(None, "date", "strip", None), P(), P()),
        out_specs=(P(None, "date", "strip"), P(None, "date", "strip")),
        check_vma=False,
    )
```
